128 devices in a mesh: dp: 16 (over z_lo, x, core), seq: 8 (over z_hi, y).
Axes of the slice: x: 4, y: 4, z: 4 (z_hi: 2, z_lo: 2; z = z_hi * 2 + z_lo), core: 2. Of those that a mesh axis runs over, the one named last changes fastest.
Arguments:
- query_all: bfloat16 [16, 2048, 3072], P('dp', 'seq'), may hold values from -6 to 6
- key_all: bfloat16 [16, 2048, 3072], P('dp', 'seq'), may hold values from -6 to 6
- value_all: bfloat16 [16, 2048, 3072], P('dp', 'seq'), may hold values from -6 to 6
- out_weight: bfloat16 [3072, 5120], P('seq'), may hold values from -0.109375 to 0.109375
- cotangent: bfloat16 [16, 1280, 5120], P('dp', 'seq'), may hold values from -6 to 6
- visible: int32 [16, 1280], P('dp', 'seq'), may hold values from 0 to 255, as said below
- counts: int32 [16, 8], P('dp'), may hold values from 96 to 160, as said below
Outputs:
- output_rows: bfloat16 [16, 1280, 5120], P('dp', 'seq')
- grad_query: bfloat16 [16, 2048, 3072], P('dp', 'seq')
- grad_key: bfloat16 [16, 2048, 3072], P('dp', 'seq')
- grad_value: bfloat16 [16, 2048, 3072], P('dp', 'seq')
- grad_weight: float32 [3072, 5120], P('seq', 'dp')
The draws below stay inside these ranges and needn't reach their ends.
Inputs may be any that keep to these rules, and one draw needn't show every extreme that they name: `counts`: in each clip one shard holds exactly 160 visible tokens. `visible`: for clip c and shard s, entries s * 160 to s * 160 + counts[c, s] - 1 are distinct token numbers within the shard in increasing order; the remaining entries of the shard are 0.
All inputs are finite; a program needn't handle non-finite values.
Results may differ from the reference program's by a relative error of at most 0.022.
Values may be sent and summed in bfloat16 or wider, within the bound.
No kernel may reach another device: no remote copies, remote signals or barrier semaphores. Data moves between devices by JAX's collectives and lax.ppermute only.
A program may use at most 192 MiB of HBM per device.

```python
import math
import jax
import jax.numpy as jnp
from jax import lax

D = 5120
HEADS = 24
HEAD_DIM = 128
TOK_SHARD = 256
CAP = 160
CHANNELS = 3072
CLIPS = 16
TOKENS_CLIP = 2048
N_SEQ = 8


def visible_counts(key):
    key = jax.random.fold_in(key, 101)
    lower = 3 * TOK_SHARD // 8
    drawn = jax.random.randint(key, (CLIPS, N_SEQ), lower, CAP + 1)
    picked = jax.random.randint(jax.random.fold_in(key, 7), (CLIPS,), 0, N_SEQ)
    drawn = jnp.where(jnp.arange(N_SEQ)[None, :] == picked[:, None], CAP, drawn)
    return drawn.astype(jnp.int32)


def draw_counts(key, part):
    return visible_counts(key)


def draw_visible(key, part):
    drawn = visible_counts(key)
    key = jax.random.fold_in(key, 5)
    several = jax.random.split(key, CLIPS * N_SEQ)
    orders = jax.vmap(lambda single: jax.random.permutation(single, TOK_SHARD)[:CAP])(several)
    orders = orders.reshape(CLIPS, N_SEQ, CAP)
    within = jnp.arange(CAP)
    alive_mask = within[None, None, :] < drawn[:, :, None]
    sort_keys = jnp.where(alive_mask, orders, TOK_SHARD + within[None, None, :])
    ordered = jnp.sort(sort_keys, axis=-1)
    result = jnp.where(alive_mask, ordered, 0)
    return result.reshape(CLIPS, N_SEQ * CAP).astype(jnp.int32)


def draw_query(key, part):
    key = jax.random.fold_in(key, 11)
    shape_full = (CLIPS, TOKENS_CLIP, HEADS * HEAD_DIM)
    base = jnp.clip(1.5 * jax.random.normal(key, shape_full, jnp.float32), -6.0, 6.0)
    return base.astype(jnp.bfloat16)


def draw_key_all(key, part):
    key = jax.random.fold_in(key, 13)
    shape_full = (CLIPS, TOKENS_CLIP, HEADS * HEAD_DIM)
    base = jnp.clip(1.5 * jax.random.normal(key, shape_full, jnp.float32), -6.0, 6.0)
    return base.astype(jnp.bfloat16)


def draw_query_all(key, part):
    return draw_query(key, part)


def block_scale(key, dims, shards, smallest, high):
    def one(axis_at, blocks):
        steps = jax.random.uniform(jax.random.fold_in(jax.random.fold_in(key, 6), axis_at), (blocks,), jnp.float32, smallest / len(shards), high / len(shards))
        return jnp.repeat(jnp.exp(steps), dims[axis_at] // blocks).reshape((-1,) + (1,) * (len(dims) - axis_at - 1))

    gain = one(*shards[0])
    for cut in shards[1:]:
        gain = gain * one(*cut)
    return gain


def normal_values(stream_key, extent, scale, bound, cuts=(), kind=jnp.bfloat16):
    entries = jax.random.normal(stream_key, extent, jnp.float32) * scale
    if len(cuts) > 0:
        entries = block_scale(stream_key, extent, cuts, -0.22, 0.18) * entries
    return jnp.clip(entries, min=-bound, max=bound).astype(kind)


def setup_inputs(seed: int = 0) -> dict:
    arg_keys = jax.random.split(jax.random.key(seed), 8)
    query_all = draw_query_all(jax.random.fold_in(arg_keys[7], 71), 0)
    key_all = draw_key_all(jax.random.fold_in(arg_keys[7], 71), 0)
    value_all = normal_values(arg_keys[2], (CLIPS, TOKENS_CLIP, CHANNELS), 1.0, 6.0, ((0, 16), (1, 8)))
    out_weight = normal_values(arg_keys[3], (CHANNELS, D), CHANNELS ** -0.5, 0.109375, ((0, 8),))
    cotangent = normal_values(arg_keys[4], (CLIPS, N_SEQ * CAP, D), 1.0, 6.0, ((0, 16), (1, 8)))
    visible = draw_visible(jax.random.fold_in(arg_keys[7], 71), 0)
    counts = draw_counts(jax.random.fold_in(arg_keys[7], 71), 0)
    return dict(query_all=query_all, key_all=key_all, value_all=value_all, out_weight=out_weight, cotangent=cotangent, visible=visible, counts=counts)


def slot_layout(visible_row, counts_row):
    position = jnp.arange(N_SEQ * CAP, dtype=jnp.int32)
    owner = position // CAP
    within = position % CAP
    matching = owner[:, None] == jnp.arange(N_SEQ, dtype=jnp.int32)[None, :]
    count_each = lax.optimization_barrier(jnp.sum(jnp.where(matching, counts_row[None, :], 0), axis=1))
    alive_mask = within < count_each
    target = (owner * TOK_SHARD + visible_row).astype(jnp.int32)
    return (target, alive_mask)

def split_heads(matrix):
    return matrix.reshape(matrix.shape[0], HEADS, HEAD_DIM).transpose(1, 0, 2).astype(jnp.float32)

def join_heads(tensor):
    return tensor.transpose(1, 0, 2).reshape(tensor.shape[1], HEADS * HEAD_DIM)

def one_clip(out_weight, grad_total, inputs):
    query_clip, key_clip, value_clip, cotangent_clip, visible_row, counts_row = inputs
    total_rows = N_SEQ * CAP
    score_scale = 1.0 / math.sqrt(HEAD_DIM)
    target, alive_mask = slot_layout(visible_row, counts_row)
    keep_rows = alive_mask.astype(jnp.bfloat16)[:, None]
    query_rows = query_clip[target] * keep_rows
    key_rows = key_clip[target] * keep_rows
    value_rows = value_clip[target] * keep_rows
    query_heads = split_heads(query_rows)
    key_heads = split_heads(key_rows)
    value_heads = split_heads(value_rows)
    scores = jnp.einsum('hqd,hkd->hqk', query_heads, key_heads) * score_scale
    masked = jnp.where(alive_mask[None, None, :], scores, -1e+30)
    row_max = lax.optimization_barrier(jnp.max(masked, axis=-1, keepdims=True))
    expo = jnp.exp(masked - row_max)
    soft = expo / lax.optimization_barrier(jnp.sum(expo, axis=-1, keepdims=True))
    soft_round = soft.astype(jnp.bfloat16)
    attn_heads = jnp.einsum('hqk,hkd->hqd', soft_round.astype(jnp.float32), value_heads)
    attn_heads = attn_heads * alive_mask.astype(jnp.float32)[None, :, None]
    attention_rows = join_heads(attn_heads).astype(jnp.bfloat16)
    group_width = HEADS * HEAD_DIM // N_SEQ
    grouped = attention_rows.reshape(total_rows, N_SEQ, group_width).astype(jnp.float32)
    weight_grouped = out_weight.reshape(N_SEQ, group_width, D).astype(jnp.float32)
    partial_terms = jnp.einsum('rnc,ncd->nrd', grouped, weight_grouped).astype(jnp.bfloat16)
    output_clip = lax.optimization_barrier(jnp.sum(partial_terms.astype(jnp.float32), axis=0)).astype(jnp.bfloat16)
    grad_attn = jnp.dot(cotangent_clip, out_weight.T, preferred_element_type=jnp.float32)
    grad_attn = (grad_attn * alive_mask.astype(jnp.float32)[:, None]).astype(jnp.bfloat16)
    grad_total = grad_total + jnp.dot(attention_rows.T, cotangent_clip, preferred_element_type=jnp.float32)
    attn_grad_heads = split_heads(grad_attn)
    grad_value_heads = jnp.einsum('hqk,hqd->hkd', soft_round.astype(jnp.float32), attn_grad_heads).astype(jnp.bfloat16)
    dsoft = jnp.einsum('hqd,hkd->hqk', attn_grad_heads, value_heads)
    delta = lax.optimization_barrier(jnp.sum(soft * dsoft, axis=-1, keepdims=True))
    dscore = (soft * (dsoft - delta) * score_scale).astype(jnp.bfloat16).astype(jnp.float32)
    grad_query_heads = jnp.einsum('hqk,hkd->hqd', dscore, key_heads).astype(jnp.bfloat16)
    grad_key_heads = jnp.einsum('hqk,hqd->hkd', dscore, query_heads).astype(jnp.bfloat16)
    empty = jnp.zeros((TOKENS_CLIP, HEADS * HEAD_DIM), jnp.bfloat16)
    grad_query_clip = empty.at[target].add(join_heads(grad_query_heads))
    grad_key_clip = empty.at[target].add(join_heads(grad_key_heads))
    grad_value_clip = empty.at[target].add(join_heads(grad_value_heads))
    return (grad_total, (output_clip, grad_query_clip, grad_key_clip, grad_value_clip))

def reference(query_all, key_all, value_all, out_weight, cotangent, visible, counts):
    start_total = jnp.zeros((HEADS * HEAD_DIM, D), jnp.float32)

    def stepper(grad_total, inputs):
        return one_clip(out_weight, grad_total, inputs)
    grad_weight, outputs = lax.scan(stepper, start_total, (query_all, key_all, value_all, cotangent, visible, counts))
    output_rows, grad_query, grad_key, grad_value = outputs
    return (output_rows, grad_query, grad_key, grad_value, grad_weight)
```

```python
import functools
import math

import jax
import jax.numpy as jnp
import numpy as np
from jax import lax
from jax.experimental import pallas as pl
from jax.experimental.pallas import tpu as pltpu
from jax.sharding import Mesh, PartitionSpec as P

HEAD_DIM = 128
HEADS = 3
GROUP = HEADS * HEAD_DIM
CAP = 160
TOK = 256
NS = 8
NX = 4
D = 5120
HALF = D // (2 * NX)
ROWS = NS * CAP
XROWS = NX * CAP
VMEM = 56 * 1024 * 1024
F32 = jnp.float32
BF16 = jnp.bfloat16
AXES = ("zl", "x", "c", "zh", "y")
SEQ = ("zh", "y")


def params(*semantics):
    return pltpu.CompilerParams(dimension_semantics=semantics, vmem_limit_bytes=VMEM)


def dot(a, b, dims):
    return lax.dot_general(a, b, (dims, ((), ())), preferred_element_type=F32)


def gather_kernel(pick_ref, q_ref, k_ref, v_ref, out_ref):
    token = lax.broadcasted_iota(jnp.int32, (CAP, TOK), 1)
    hot = (token == pick_ref[...]).astype(F32).astype(BF16)
    for i, ref in enumerate((q_ref, k_ref, v_ref)):
        out_ref[0, i] = dot(hot, ref[...], ((1,), (0,))).astype(BF16)


def gather_rows(pick, q, k, v):
    block = pl.BlockSpec((TOK, GROUP), lambda s: (0, s))
    return pl.pallas_call(
        gather_kernel,
        grid=(NS,),
        in_specs=[pl.BlockSpec((CAP, 1), lambda s: (0, 0)), block, block, block],
        out_specs=pl.BlockSpec((1, 3, CAP, GROUP), lambda s: (s, 0, 0, 0)),
        out_shape=jax.ShapeDtypeStruct((NS, 3, CAP, GROUP), BF16),
        compiler_params=params("arbitrary"),
        cost_estimate=pl.CostEstimate(flops=2 * 3 * CAP * TOK * GROUP * NS, bytes_accessed=8 << 20, transcendentals=0),
    )(pick, q, k, v)


def scatter_kernel(pick_ref, rows_ref, q_ref, k_ref, v_ref):
    token = lax.broadcasted_iota(jnp.int32, (TOK, CAP), 0)
    hot = (token == pick_ref[...]).astype(F32).astype(BF16)
    for i, ref in enumerate((q_ref, k_ref, v_ref)):
        ref[...] = dot(hot, rows_ref[0, i], ((1,), (0,))).astype(BF16)


def scatter_rows(pick, rows):
    block = pl.BlockSpec((TOK, GROUP), lambda s: (0, s))
    return pl.pallas_call(
        scatter_kernel,
        grid=(NS,),
        in_specs=[
            pl.BlockSpec((1, CAP), lambda s: (0, 0)),
            pl.BlockSpec((1, 3, CAP, GROUP), lambda s: (s, 0, 0, 0)),
        ],
        out_specs=[block] * 3,
        out_shape=[jax.ShapeDtypeStruct((TOK, NS * GROUP), BF16)] * 3,
        compiler_params=params("arbitrary"),
        cost_estimate=pl.CostEstimate(flops=2 * 3 * CAP * TOK * GROUP * NS, bytes_accessed=8 << 20, transcendentals=0),
    )(pick, rows)


QB = 2
NQ = NS // QB


def forward_kernel(bias_ref, live_ref, q_ref, k_ref, v_ref, attn_ref, soft_ref):
    scale = math.log2(math.e) / math.sqrt(HEAD_DIM)
    keys = k_ref[...].reshape(ROWS, HEAD_DIM)
    values = v_ref[...].reshape(ROWS, HEAD_DIM)
    bias = bias_ref[...]
    for j in range(QB):
        scores = dot(q_ref[j, 0], keys, ((1,), (1,))) + bias
        top = jnp.max(scores, axis=1, keepdims=True)
        expo = jnp.exp2((scores - top) * scale)
        soft = (expo * (1.0 / jnp.sum(expo, axis=1, keepdims=True))).astype(BF16)
        soft_ref[0, j * CAP : (j + 1) * CAP, :] = soft
        attn_ref[j] = (dot(soft, values, ((1,), (0,))) * live_ref[j]).astype(BF16)


def forward(bias, live, qkv):
    def part(i, rows):
        if rows == QB:
            return pl.BlockSpec((QB, 1, CAP, HEAD_DIM), lambda h, r: (r, i, 0, h))
        return pl.BlockSpec((NS, 1, CAP, HEAD_DIM), lambda h, r: (0, i, 0, h))

    return pl.pallas_call(
        forward_kernel,
        grid=(HEADS, NQ),
        in_specs=[
            pl.BlockSpec((1, ROWS), lambda h, r: (0, 0)),
            pl.BlockSpec((QB, CAP, 1), lambda h, r: (r, 0, 0)),
            part(0, QB),
            part(1, NS),
            part(2, NS),
        ],
        out_specs=[
            pl.BlockSpec((QB, CAP, HEAD_DIM), lambda h, r: (r, 0, h)),
            pl.BlockSpec((1, QB * CAP, ROWS), lambda h, r: (h, r, 0)),
        ],
        out_shape=[
            jax.ShapeDtypeStruct((NS, CAP, GROUP), BF16),
            jax.ShapeDtypeStruct((HEADS, ROWS, ROWS), BF16),
        ],
        compiler_params=params("arbitrary", "arbitrary"),
        cost_estimate=pl.CostEstimate(flops=8 * ROWS * ROWS * GROUP, bytes_accessed=14 << 20, transcendentals=HEADS * ROWS * ROWS),
    )(bias, live, qkv, qkv, qkv)


def backward_kernel(live_ref, q_ref, k_ref, v_ref, grad_ref, soft_ref, out_ref, gk_ref, gv_ref):
    r = pl.program_id(1)
    scale = 1.0 / math.sqrt(HEAD_DIM)
    keys = k_ref[...].reshape(ROWS, HEAD_DIM)
    values = v_ref[...].reshape(ROWS, HEAD_DIM)

    @pl.when(r == 0)
    def _():
        gk_ref[...] = jnp.zeros_like(gk_ref)
        gv_ref[...] = jnp.zeros_like(gv_ref)

    for j in range(QB):
        grad = (grad_ref[j].astype(F32) * live_ref[j]).astype(BF16)
        soft_b = soft_ref[0, j * CAP : (j + 1) * CAP, :]
        soft = soft_b.astype(F32)
        dsoft = dot(grad, values, ((1,), (1,)))
        delta = jnp.sum(soft * dsoft, axis=1, keepdims=True)
        dscore = (soft * ((dsoft - delta) * scale)).astype(BF16)
        out_ref[r * QB + j, 0] = dot(dscore, keys, ((1,), (0,))).astype(BF16)
        gv_ref[...] += dot(grad, soft_b, ((0,), (0,)))
        gk_ref[...] += dot(q_ref[j, 0], dscore, ((0,), (0,)))

    @pl.when(r == NQ - 1)
    def _():
        out_ref[:, 1] = gk_ref[...].T.astype(BF16).reshape(NS, CAP, HEAD_DIM)
        out_ref[:, 2] = gv_ref[...].T.astype(BF16).reshape(NS, CAP, HEAD_DIM)


def backward(live, qkv, grad, soft):
    def part(i, rows):
        if rows == QB:
            return pl.BlockSpec((QB, 1, CAP, HEAD_DIM), lambda h, r: (r, i, 0, h))
        return pl.BlockSpec((NS, 1, CAP, HEAD_DIM), lambda h, r: (0, i, 0, h))

    return pl.pallas_call(
        backward_kernel,
        grid=(HEADS, NQ),
        in_specs=[
            pl.BlockSpec((QB, CAP, 1), lambda h, r: (r, 0, 0)),
            part(0, QB),
            part(1, NS),
            part(2, NS),
            pl.BlockSpec((QB, CAP, HEAD_DIM), lambda h, r: (r, 0, h)),
            pl.BlockSpec((1, QB * CAP, ROWS), lambda h, r: (h, r, 0)),
        ],
        out_specs=pl.BlockSpec((NS, 3, CAP, HEAD_DIM), lambda h, r: (0, 0, 0, h)),
        out_shape=jax.ShapeDtypeStruct((NS, 3, CAP, GROUP), BF16),
        scratch_shapes=[pltpu.VMEM((HEAD_DIM, ROWS), F32), pltpu.VMEM((HEAD_DIM, ROWS), F32)],
        compiler_params=params("arbitrary", "arbitrary"),
        cost_estimate=pl.CostEstimate(flops=16 * ROWS * ROWS * GROUP, bytes_accessed=18 << 20, transcendentals=0),
    )(live, qkv, qkv, qkv, grad, soft)


def split_kernel(core_ref, in_ref, out_ref):
    out_ref[0, 0] = in_ref[...]


def split_columns(core, rows):
    return pl.pallas_call(
        split_kernel,
        grid_spec=pltpu.PrefetchScalarGridSpec(
            num_scalar_prefetch=1,
            grid=(NX, 2),
            in_specs=[pl.BlockSpec((CAP, HALF), lambda x, h, core: (0, (h ^ core[0]) * NX + x))],
            out_specs=pl.BlockSpec((1, 1, CAP, HALF), lambda x, h, core: (x, h, 0, 0)),
        ),
        out_shape=jax.ShapeDtypeStruct((NX, 2, CAP, HALF), BF16),
        compiler_params=params("arbitrary", "arbitrary"),
        cost_estimate=pl.CostEstimate(flops=0, bytes_accessed=4 * CAP * D, transcendentals=0),
    )(core, rows)


def join_kernel(core_ref, in_ref, out_ref):
    out_ref[...] = in_ref[0, 0]


def join_columns(core, blocks):
    return pl.pallas_call(
        join_kernel,
        grid_spec=pltpu.PrefetchScalarGridSpec(
            num_scalar_prefetch=1,
            grid=(NX, 2),
            in_specs=[pl.BlockSpec((1, 1, CAP, HALF), lambda x, h, core: (x, h, 0, 0))],
            out_specs=pl.BlockSpec((CAP, HALF), lambda x, h, core: (0, (h ^ core[0]) * NX + x)),
        ),
        out_shape=jax.ShapeDtypeStruct((CAP, D), BF16),
        compiler_params=params("arbitrary", "arbitrary"),
        cost_estimate=pl.CostEstimate(flops=0, bytes_accessed=4 * CAP * D, transcendentals=0),
    )(core, blocks)


def grad_attn_kernel(cot_ref, own_ref, oth_ref, out_ref):
    own = cot_ref[:, 0].reshape(XROWS, HALF)
    oth = cot_ref[:, 1].reshape(XROWS, HALF)
    total = dot(own, own_ref[0], ((1,), (1,))) + dot(oth, oth_ref[0], ((1,), (1,)))
    out_ref[:, 0] = total.astype(BF16).reshape(NX, CAP, GROUP)


def grad_attn_part(cot, own, oth):
    weight = pl.BlockSpec((1, GROUP, HALF), lambda s: (s, 0, 0))
    return pl.pallas_call(
        grad_attn_kernel,
        grid=(NS,),
        in_specs=[pl.BlockSpec((NX, 2, CAP, HALF), lambda s: (0, 0, 0, 0)), weight, weight],
        out_specs=pl.BlockSpec((NX, 1, CAP, GROUP), lambda s: (0, s, 0, 0)),
        out_shape=jax.ShapeDtypeStruct((NX, NS, CAP, GROUP), BF16),
        compiler_params=params("arbitrary"),
        cost_estimate=pl.CostEstimate(flops=4 * XROWS * HALF * NS * GROUP, bytes_accessed=14 << 20, transcendentals=0),
    )(cot, own, oth)


def dense_kernel(core_ref, attn_ref, cot_ref, own_ref, oth_ref, out_ref, keep_ref, send_ref, acc_ref, turn_ref):
    s = pl.program_id(0)
    core = core_ref[0]
    third = HALF // 2

    @pl.when(s == 0)
    def _():
        acc_ref[...] = jnp.zeros_like(acc_ref)
        for h in range(2):
            turned = cot_ref[:, h].reshape(XROWS, HALF).T
            for c in range(2):
                rows = turned[c * third : (c + 1) * third]
                turn_ref[c ^ core, h ^ core] = rows

    rows = attn_ref[:, 0].reshape(XROWS, GROUP)
    acc_ref[0] += dot(rows, own_ref[0], ((1,), (0,)))
    acc_ref[1] += dot(rows, oth_ref[0], ((1,), (0,)))
    for zl in range(2):
        keep_ref[zl, 0] = dot(turn_ref[0, zl], rows, ((1,), (0,))).astype(BF16)
        send_ref[zl, 0] = dot(turn_ref[1, zl], rows, ((1,), (0,))).astype(BF16)

    @pl.when(s == NS - 1)
    def _():
        for h in range(2):
            out_ref[:, h] = acc_ref[h].astype(BF16).reshape(NX, CAP, HALF)


def dense(core, attn, cot, own, oth):
    weight = pl.BlockSpec((1, GROUP, HALF), lambda s, core: (s, 0, 0))
    wide = pl.BlockSpec((NX, 2, CAP, HALF), lambda s, core: (0, 0, 0, 0))
    grad = pl.BlockSpec((2, 1, HALF // 2, GROUP), lambda s, core: (0, s, 0, 0))
    return pl.pallas_call(
        dense_kernel,
        grid_spec=pltpu.PrefetchScalarGridSpec(
            num_scalar_prefetch=1,
            grid=(NS,),
            in_specs=[pl.BlockSpec((NX, 1, CAP, GROUP), lambda s, core: (0, s, 0, 0)), wide, weight, weight],
            out_specs=[wide, grad, grad],
            scratch_shapes=[
                pltpu.VMEM((2, XROWS, HALF), F32),
                pltpu.VMEM((2, 2, HALF // 2, XROWS), BF16),
            ],
        ),
        out_shape=[
            jax.ShapeDtypeStruct((NX, 2, CAP, HALF), BF16),
            jax.ShapeDtypeStruct((2, NS, HALF // 2, GROUP), BF16),
            jax.ShapeDtypeStruct((2, NS, HALF // 2, GROUP), BF16),
        ],
        compiler_params=params("arbitrary"),
        cost_estimate=pl.CostEstimate(flops=8 * XROWS * HALF * NS * GROUP, bytes_accessed=26 << 20, transcendentals=0),
    )(core, attn, cot, own, oth)


def other_core(value, n_dp):
    return lax.ppermute(value, ("zl", "x", "c"), [(i, i ^ 1) for i in range(n_dp)])


def swap(value, axes):
    return lax.all_to_all(value, axes, split_axis=0, concat_axis=0, tiled=True)


def on_device(query_all, key_all, value_all, out_weight, cotangent, visible, counts):
    n_dp = 4 * NX
    x = lax.axis_index("x")
    core = lax.axis_index("c")
    core_arg = core.astype(jnp.int32).reshape(1)
    place = lax.axis_index(SEQ)

    slots = jnp.arange(CAP, dtype=jnp.int32)
    alive_all = slots[None, :] < counts[0][:, None]
    own_count = jnp.sum(jnp.where(jnp.arange(NS, dtype=jnp.int32) == place, counts[0], 0))
    pick = jnp.where(slots < own_count, visible[0], -1)
    bias = jnp.where(alive_all, 0.0, -1e30).astype(F32).reshape(1, ROWS)
    live = alive_all.astype(F32)[:, :, None]

    mine = lax.dynamic_slice(out_weight, (0, core * (NX * HALF) + x * HALF), (GROUP, HALF))
    own = lax.all_gather(mine, SEQ, axis=0, tiled=False)
    oth = other_core(own, n_dp)

    qkv = swap(gather_rows(pick[:, None], query_all[0], key_all[0], value_all[0]), SEQ)
    cot = swap(split_columns(core_arg, cotangent[0]), "x")

    attn, soft = forward(bias, live, qkv)
    attn = swap(attn, SEQ)
    attn_x = lax.all_gather(attn, "x", axis=0, tiled=False)

    grad_part = grad_attn_part(cot, own, oth)
    grad_attn = lax.psum_scatter(grad_part, "x", scatter_dimension=0, tiled=False)
    grad_attn = swap(grad_attn, SEQ)

    out, keep, send = dense(core_arg, attn_x, cot, own, oth)
    output = join_columns(core_arg, swap(out, "x"))
    weight_part = (keep.astype(F32) + other_core(send, n_dp).astype(F32)).astype(BF16)
    weight_part = weight_part.reshape(2 * NS, HALF // 2, GROUP)
    grad_weight = lax.psum_scatter(weight_part, ("zl",) + SEQ, scatter_dimension=0, tiled=False)
    grad_weight = grad_weight.astype(F32).T

    grads = swap(backward(live, qkv, grad_attn, soft), SEQ)
    grad_query, grad_key, grad_value = scatter_rows(pick[None, :], grads)
    return (output[None], grad_query[None], grad_key[None], grad_value[None], grad_weight)


def solution(mesh):
    fine = Mesh(np.asarray(mesh.devices).reshape(2, NX, 2, 2, 4), AXES)
    dp = ("zl", "x", "c")
    return jax.shard_map(
        on_device,
        mesh=fine,
        in_specs=(
            P(dp, SEQ, None),
            P(dp, SEQ, None),
            P(dp, SEQ, None),
            P(SEQ, None),
            P(dp, SEQ, None),
            P(dp, SEQ),
            P(dp, None),
        ),
        out_specs=(
            P(dp, SEQ, None),
            P(dp, SEQ, None),
            P(dp, SEQ, None),
            P(dp, SEQ, None),
            P(SEQ, dp),
        ),
        check_vma=False,
    )
```

```python
import functools
import math

import jax
import jax.numpy as jnp
import numpy as np
from jax import lax
from jax.experimental import pallas as pl
from jax.experimental.pallas import tpu as pltpu
from jax.sharding import Mesh, PartitionSpec as P

HEAD_DIM = 128
HEADS = 3
GROUP = HEADS * HEAD_DIM
CAP = 160
TOK = 256
NS = 8
NX = 4
D = 5120
HALF = D // (2 * NX)
ROWS = NS * CAP
XROWS = NX * CAP
VMEM = 56 * 1024 * 1024
F32 = jnp.float32
BF16 = jnp.bfloat16
BRIEF = pl.CostEstimate(flops=1, bytes_accessed=1, transcendentals=0)
LONG = pl.CostEstimate(flops=2 * 10**11, bytes_accessed=1, transcendentals=0)
AXES = ("zl", "x", "c", "zh", "y")
SEQ = ("zh", "y")


def params(*semantics):
    return pltpu.CompilerParams(dimension_semantics=semantics, vmem_limit_bytes=VMEM)


def dot(a, b, dims):
    return lax.dot_general(a, b, (dims, ((), ())), preferred_element_type=F32)


def gather_kernel(pick_ref, q_ref, k_ref, v_ref, out_ref):
    token = lax.broadcasted_iota(jnp.int32, (CAP, TOK), 1)
    hot = (token == pick_ref[...]).astype(F32).astype(BF16)
    for i, ref in enumerate((q_ref, k_ref, v_ref)):
        out_ref[0, i] = dot(hot, ref[...], ((1,), (0,))).astype(BF16)


def gather_rows(pick, q, k, v):
    block = pl.BlockSpec((TOK, GROUP), lambda s: (0, s))
    return pl.pallas_call(
        gather_kernel,
        grid=(NS,),
        in_specs=[pl.BlockSpec((CAP, 1), lambda s: (0, 0)), block, block, block],
        out_specs=pl.BlockSpec((1, 3, CAP, GROUP), lambda s: (s, 0, 0, 0)),
        out_shape=jax.ShapeDtypeStruct((NS, 3, CAP, GROUP), BF16),
        compiler_params=params("arbitrary"),
        cost_estimate=BRIEF,
    )(pick, q, k, v)


def scatter_kernel(pick_ref, first_ref, rest_ref, q_ref, k_ref, v_ref):
    token = lax.broadcasted_iota(jnp.int32, (TOK, CAP), 0)
    hot = (token == pick_ref[...]).astype(F32).astype(BF16)
    for i, ref in enumerate((q_ref, k_ref, v_ref)):
        rows = jnp.concatenate([first_ref[0, i], rest_ref[0, i]], axis=1)
        ref[...] = dot(hot, rows, ((1,), (0,))).astype(BF16)


def scatter_rows(pick, first, rest):
    block = pl.BlockSpec((TOK, GROUP), lambda s: (0, s))
    return pl.pallas_call(
        scatter_kernel,
        grid=(NS,),
        in_specs=[
            pl.BlockSpec((1, CAP), lambda s: (0, 0)),
            pl.BlockSpec((1, 3, CAP, GROUP - HEAD_DIM), lambda s: (s, 0, 0, 0)),
            pl.BlockSpec((1, 3, CAP, HEAD_DIM), lambda s: (s, 0, 0, 0)),
        ],
        out_specs=[block] * 3,
        out_shape=[jax.ShapeDtypeStruct((TOK, NS * GROUP), BF16)] * 3,
        compiler_params=params("arbitrary"),
        cost_estimate=BRIEF,
    )(pick, first, rest)


QB = 4
NQ = NS // QB
COLUMN = pl.BlockSpec((QB, CAP, 1), lambda h, r: (r, 0, 0))
HEAD_COLUMN = pl.BlockSpec((1, QB, CAP, 1), lambda h, r: (h, r, 0, 0))
HEAD_ROWS = pl.BlockSpec((QB, CAP, HEAD_DIM), lambda h, r: (r, 0, h))
HEAD_SQUARE = pl.BlockSpec((1, QB * CAP, ROWS), lambda h, r: (h, r, 0))


def some_rows(i):
    return pl.BlockSpec((QB, 1, CAP, HEAD_DIM), lambda h, r: (r, i, 0, h))


def all_rows(i):
    return pl.BlockSpec((NS, 1, CAP, HEAD_DIM), lambda h, r: (0, i, 0, h))


def forward_kernel(bias_ref, live_ref, q_ref, k_ref, v_ref, attn_ref, expo_ref, inv_ref):
    scale = math.log2(math.e) / math.sqrt(HEAD_DIM)
    keys = k_ref[...].reshape(ROWS, HEAD_DIM)
    values = v_ref[...].reshape(ROWS, HEAD_DIM)
    bias = bias_ref[...]
    for j in range(QB):
        scores = dot(q_ref[j, 0], keys, ((1,), (1,))) + bias
        top = jnp.max(scores, axis=1, keepdims=True)
        expo = jnp.exp2((scores - top) * scale)
        inv = 1.0 / jnp.sum(expo, axis=1, keepdims=True)
        expo = expo.astype(BF16)
        expo_ref[0, j * CAP : (j + 1) * CAP, :] = expo
        inv_ref[0, j] = inv
        attn_ref[j] = (dot(expo, values, ((1,), (0,))) * (inv * live_ref[j])).astype(BF16)


def forward(bias, live, qkv):
    return pl.pallas_call(
        forward_kernel,
        grid=(HEADS, NQ),
        in_specs=[pl.BlockSpec((1, ROWS), lambda h, r: (0, 0)), COLUMN, some_rows(0), all_rows(1), all_rows(2)],
        out_specs=[HEAD_ROWS, HEAD_SQUARE, HEAD_COLUMN],
        out_shape=[
            jax.ShapeDtypeStruct((NS, CAP, GROUP), BF16),
            jax.ShapeDtypeStruct((HEADS, ROWS, ROWS), BF16),
            jax.ShapeDtypeStruct((HEADS, NS, CAP, 1), F32),
        ],
        compiler_params=params("arbitrary", "arbitrary"),
        cost_estimate=LONG,
    )(bias, live, qkv, qkv, qkv)


def backward_kernel(live_ref, q_ref, k_ref, v_ref, grad_ref, expo_ref, inv_ref, out_ref, gk_ref, gv_ref):
    r = pl.program_id(1)
    scale = 1.0 / math.sqrt(HEAD_DIM)
    keys = k_ref[...].reshape(ROWS, HEAD_DIM)
    values = v_ref[...].reshape(ROWS, HEAD_DIM)

    @pl.when(r == 0)
    def _():
        gk_ref[...] = jnp.zeros_like(gk_ref)
        gv_ref[...] = jnp.zeros_like(gv_ref)

    for j in range(QB):
        inv = inv_ref[0, j]
        grad = (grad_ref[j].astype(F32) * live_ref[j]).astype(BF16)
        expo_b = expo_ref[0, j * CAP : (j + 1) * CAP, :]
        expo = expo_b.astype(F32)
        dsoft = dot(grad, values, ((1,), (1,)))
        delta = jnp.sum(expo * dsoft, axis=1, keepdims=True) * inv
        dscore = (expo * ((dsoft - delta) * (inv * scale))).astype(BF16)
        out_ref[r * QB + j, 0] = dot(dscore, keys, ((1,), (0,))).astype(BF16)
        gv_ref[...] += dot((grad.astype(F32) * inv).astype(BF16), expo_b, ((0,), (0,)))
        gk_ref[...] += dot(q_ref[j, 0], dscore, ((0,), (0,)))

    @pl.when(r == NQ - 1)
    def _():
        out_ref[:, 1] = gk_ref[...].T.astype(BF16).reshape(NS, CAP, HEAD_DIM)
        out_ref[:, 2] = gv_ref[...].T.astype(BF16).reshape(NS, CAP, HEAD_DIM)


def backward(live, qkv, grad, expo, inv, first, count):
    def at(spec, axis):
        def index(h, r):
            place = list(spec.index_map(h, r))
            place[axis] = place[axis] + first
            return tuple(place)

        return pl.BlockSpec(spec.block_shape, index)

    rows = at(HEAD_ROWS, 2)
    return pl.pallas_call(
        backward_kernel,
        grid=(count, NQ),
        in_specs=[
            COLUMN,
            at(some_rows(0), 3),
            at(all_rows(1), 3),
            at(all_rows(2), 3),
            rows,
            at(HEAD_SQUARE, 0),
            at(HEAD_COLUMN, 0),
        ],
        out_specs=pl.BlockSpec((NS, 3, CAP, HEAD_DIM), lambda h, r: (0, 0, 0, h)),
        out_shape=jax.ShapeDtypeStruct((NS, 3, CAP, count * HEAD_DIM), BF16),
        scratch_shapes=[pltpu.VMEM((HEAD_DIM, ROWS), F32), pltpu.VMEM((HEAD_DIM, ROWS), F32)],
        compiler_params=params("arbitrary", "arbitrary"),
        cost_estimate=LONG,
    )(live, qkv, qkv, qkv, grad, expo, inv)


def column(place_ref, x, h):
    block = (h ^ place_ref[1]) * NX + x
    return pl.ds(pl.multiple_of(block * HALF, HALF), HALF)


def split_kernel(place_ref, in_ref, out_ref):
    for x in range(NX):
        for h in range(2):
            out_ref[x, h] = in_ref[:, column(place_ref, x, h)]


SMEM = pl.BlockSpec(memory_space=pltpu.SMEM)


def split_columns(place, rows):
    return pl.pallas_call(
        split_kernel,
        in_specs=[SMEM, pl.BlockSpec(memory_space=pltpu.VMEM)],
        out_specs=pl.BlockSpec(memory_space=pltpu.VMEM),
        out_shape=jax.ShapeDtypeStruct((NX, 2, CAP, HALF), BF16),
        compiler_params=params(),
        cost_estimate=BRIEF,
    )(place, rows)


def join_kernel(place_ref, in_ref, out_ref):
    for x in range(NX):
        for h in range(2):
            out_ref[:, column(place_ref, x, h)] = in_ref[x, h]


def join_columns(place, blocks):
    return pl.pallas_call(
        join_kernel,
        in_specs=[SMEM, pl.BlockSpec(memory_space=pltpu.VMEM)],
        out_specs=pl.BlockSpec(memory_space=pltpu.VMEM),
        out_shape=jax.ShapeDtypeStruct((CAP, D), BF16),
        compiler_params=params(),
        cost_estimate=BRIEF,
    )(place, blocks)


def x_exchange(blocks):
    return lax.all_to_all(blocks, "x", split_axis=0, concat_axis=0, tiled=True)


def whole_block(shape):
    return pl.BlockSpec(shape, lambda s, place: (0,) * len(shape))


LOW = GROUP // 2
UPPER = pl.BlockSpec((1, LOW, HALF), lambda s, place: (s, 0, 0))
LOWER = pl.BlockSpec((2, 1, LOW, HALF), lambda s, place: (0, s, 0, 0))
PAIR = pl.BlockSpec((NX, 2, 1, CAP, GROUP), lambda s, place: (0, 0, s, 0, 0))


def weight_rows(up, far, low):
    return jnp.concatenate([up[0], low[0, 0], far[0], low[1, 0]], axis=0)


def grad_attn_kernel(place_ref, in_ref, u0, f0, l0, u1, f1, l1, out_ref, cot_ref):
    @pl.when(pl.program_id(0) == 0)
    def _():
        for j in range(NX):
            for h in range(2):
                cot_ref[h, j * CAP : (j + 1) * CAP] = in_ref[j, h]

    total = dot(cot_ref[0], weight_rows(u0, f0, l0), ((1,), (1,)))
    total = (total + dot(cot_ref[1], weight_rows(u1, f1, l1), ((1,), (1,)))).astype(BF16)
    for j in range(NX):
        for i in range(2):
            part = total[j * CAP : (j + 1) * CAP, i * GROUP : (i + 1) * GROUP]
            out_ref[j, place_ref[2] ^ i, 0] = part


def grad_attn_part(place, cot, pieces):
    return pl.pallas_call(
        grad_attn_kernel,
        grid_spec=pltpu.PrefetchScalarGridSpec(
            num_scalar_prefetch=1,
            grid=(NS // 2,),
            in_specs=[whole_block((NX, 2, CAP, HALF))] + [UPPER, UPPER, LOWER] * 2,
            out_specs=PAIR,
            scratch_shapes=[pltpu.VMEM((2, XROWS, HALF), BF16)],
        ),
        out_shape=jax.ShapeDtypeStruct((NX, 2, NS // 2, CAP, GROUP), BF16),
        compiler_params=params("arbitrary"),
        cost_estimate=LONG,
    )(place, cot, *pieces).reshape(NX, NS, CAP, GROUP)


def ring_rows(ref, i):
    return ref[:, i, 0].reshape(XROWS, GROUP)


PIECE = HALF // 4


def weight_kernel(place_ref, attn_ref, cot_ref, keep_ref, send_ref, turn_ref):
    core = place_ref[1]

    @pl.when(pl.program_id(0) == 0)
    def _():
        for h in range(2):
            for j in range(NX):
                turned = cot_ref[j, h].T
                for c in range(2):
                    part = turned[2 * c * PIECE : 2 * (c + 1) * PIECE]
                    turn_ref[c ^ core, h ^ core, :, j * CAP : (j + 1) * CAP] = part

    rows = jnp.concatenate([ring_rows(attn_ref, i) for i in range(2)], axis=1)
    for other, ref in enumerate((keep_ref, send_ref)):
        for zl in range(2):
            total = dot(turn_ref[other, zl], rows, ((1,), (0,))).astype(BF16)
            for i in range(2):
                for p in range(2):
                    ref[p, zl, i, 0] = total[p * PIECE : (p + 1) * PIECE, i * GROUP : (i + 1) * GROUP]


def weight_part(place, attn, cot):
    grad = pl.BlockSpec((2, 2, 2, 1, PIECE, GROUP), lambda s, place: (0, 0, 0, s, 0, 0))
    return pl.pallas_call(
        weight_kernel,
        grid_spec=pltpu.PrefetchScalarGridSpec(
            num_scalar_prefetch=1,
            grid=(NS // 2,),
            in_specs=[PAIR, whole_block((NX, 2, CAP, HALF))],
            out_specs=[grad, grad],
            scratch_shapes=[pltpu.VMEM((2, 2, 2 * PIECE, XROWS), BF16)],
        ),
        out_shape=[jax.ShapeDtypeStruct((2, 2, 2, NS // 2, PIECE, GROUP), BF16)] * 2,
        compiler_params=params("arbitrary"),
        cost_estimate=BRIEF,
    )(place, attn, cot)


def out_kernel(place_ref, attn_ref, u0, f0, l0, u1, f1, l1, out_ref, acc_ref):
    s = pl.program_id(0)

    @pl.when(s == 0)
    def _():
        acc_ref[...] = jnp.zeros_like(acc_ref)

    rows = jnp.concatenate([ring_rows(attn_ref, place_ref[2] ^ i) for i in range(2)], axis=1)
    acc_ref[0] += dot(rows, weight_rows(u0, f0, l0), ((1,), (0,)))
    acc_ref[1] += dot(rows, weight_rows(u1, f1, l1), ((1,), (0,)))

    @pl.when(s == NS // 2 - 1)
    def _():
        for j in range(NX):
            for h in range(2):
                out_ref[j, h] = acc_ref[h, j * CAP : (j + 1) * CAP].astype(BF16)


def out_part(place, attn, pieces):
    return pl.pallas_call(
        out_kernel,
        grid_spec=pltpu.PrefetchScalarGridSpec(
            num_scalar_prefetch=1,
            grid=(NS // 2,),
            in_specs=[PAIR] + [UPPER, UPPER, LOWER] * 2,
            out_specs=whole_block((NX, 2, CAP, HALF)),
            scratch_shapes=[pltpu.VMEM((2, XROWS, HALF), F32)],
        ),
        out_shape=jax.ShapeDtypeStruct((NX, 2, CAP, HALF), BF16),
        compiler_params=params("arbitrary"),
        cost_estimate=LONG,
    )(place, attn, *pieces)


def other_core(value):
    return lax.ppermute(value, "c", [(0, 1), (1, 0)])


def swap(value):
    return lax.all_to_all(value, SEQ, split_axis=0, concat_axis=0, tiled=True)


def after(value, *others):
    return lax.optimization_barrier((value,) + others)[0]


def along_y(value, k):
    return lax.ppermute(value, "y", [(p, (p + k) % 4) for p in range(4)])


def along_z(value, k):
    index = [0, 2, 1, 3]
    return lax.ppermute(value, ("zl", "zh"), [(index[z], index[(z + k) % 4]) for z in range(4)])


def next_half(value):
    return lax.ppermute(value, ("zl", "zh"), [(0, 3), (3, 0), (2, 1), (1, 2)])


def add(values):
    return functools.reduce(jnp.add, [v.astype(F32) for v in values])


def projection(out_weight, x, core, y, rows):
    mine = lax.dynamic_slice(out_weight, (0, core * (NX * HALF) + x * HALF), (GROUP, HALF))

    def gather(value):
        parts = [value] + [along_y(value, k) for k in (1, 3, 2)]
        zero = jnp.zeros((4,) + value.shape, BF16)
        for k, part in zip((0, -1, 1, 2), parts):
            zero = lax.dynamic_update_slice_in_dim(zero, part[None], (y + k) % 4, 0)
        return zero

    up = gather(mine[:LOW])
    low = jnp.stack([mine[LOW:], next_half(mine[LOW:])])
    up, low, rows = lax.optimization_barrier((up, low, rows))
    far = next_half(up)
    low = jnp.moveaxis(gather(low), 0, 1)
    return [up, far, low], rows


def cut_kernel(place_ref, keep_ref, got_ref, z0, z1, z2, z3, y0, y1, y2, y3):
    for k, (z_ref, y_ref) in enumerate(zip((z0, z1, z2, z3), (y0, y1, y2, y3))):
        z = lax.rem(2 * place_ref[2] + place_ref[4] + k, 4)
        zl, zh, y = lax.rem(z, 2), z // 2, lax.rem(place_ref[3] + k, 4)
        z_ref[...] = (keep_ref[0, zl, zh].astype(F32) + got_ref[0, zl, zh].astype(F32)).astype(BF16)
        for i in range(2):
            for j in range(2):
                y_ref[i, j] = (keep_ref[1, i, j, y].astype(F32) + got_ref[1, i, j, y].astype(F32)).astype(BF16)


def cut_pieces(place, keep, got):
    vmem = pl.BlockSpec(memory_space=pltpu.VMEM)
    out = pl.pallas_call(
        cut_kernel,
        in_specs=[SMEM, vmem, vmem],
        out_specs=[vmem] * 8,
        out_shape=[jax.ShapeDtypeStruct((4, PIECE, GROUP), BF16)] * 4
        + [jax.ShapeDtypeStruct((2, 2, PIECE, GROUP), BF16)] * 4,
        compiler_params=params(),
        cost_estimate=BRIEF,
    )(place, keep, got)
    return out[:4], out[4:]


def ring(along, parts):
    return add([parts[0]] + [along(parts[k], k) for k in (1, 3, 2)])


def second_phase(first, second, place):
    zh, y, zl = place[2], place[3], place[4]
    first = [lax.dynamic_index_in_dim(first, (y + k) % 4, 0, keepdims=False) for k in range(4)]
    z = [(2 * zh + zl + k) % 4 for k in range(4)]
    second = [lax.dynamic_slice(second, (k % 2, k // 2, 0, 0), (1, 1, PIECE, GROUP))[0, 0] for k in z]
    return jnp.concatenate([ring(along_y, first), ring(along_z, second)])


def on_device(query_all, key_all, value_all, out_weight, cotangent, visible, counts):
    x, core, zh, y, zl = [lax.axis_index(a).astype(jnp.int32) for a in ("x", "c", "zh", "y", "zl")]
    place = jnp.stack([x, core, zh, y, zl])
    shard = 4 * zh + y

    slots = jnp.arange(CAP, dtype=jnp.int32)
    alive_all = slots[None, :] < counts[0][:, None]
    own_count = jnp.sum(jnp.where(jnp.arange(NS, dtype=jnp.int32) == shard, counts[0], 0))
    pick = jnp.where(slots < own_count, visible[0], -1)
    bias = jnp.where(alive_all, 0.0, -1e30).astype(F32).reshape(1, ROWS)
    live = alive_all.astype(F32)[:, :, None]

    rows = gather_rows(pick[:, None], query_all[0], key_all[0], value_all[0])
    own, rows = projection(out_weight, x, core, y, rows)
    cot = x_exchange(split_columns(place, after(cotangent[0], rows)))
    own = [after(v, cot) for v in own]
    qkv = swap(after(rows, cot, *own))
    pieces = own + [other_core(v) for v in own]
    grad_part = grad_attn_part(place, cot, pieces)
    grad_attn = swap(lax.psum_scatter(grad_part, "x", scatter_dimension=0, tiled=False))

    attn, expo, inv = forward(bias, live, after(qkv, grad_part))
    attn = lax.all_gather(swap(attn), "x", axis=0, tiled=False).reshape(NX, 2, NS // 2, CAP, GROUP)

    head_grads = backward(live, qkv, grad_attn, expo, inv, 0, HEADS - 1)
    grads = backward(after(live, head_grads), qkv, grad_attn, expo, inv, HEADS - 1, 1)
    keep, send = weight_part(place, after(attn, grads), cot)
    head_grads = swap(head_grads)
    grads = swap(grads)
    first, second = cut_pieces(place, keep, other_core(after(send, head_grads)))
    token_grads = scatter_rows(pick[None, :], head_grads, grads)
    out = out_part(place, after(attn, *first, *second, *token_grads), pieces)
    first, second = ring(along_z, first).astype(BF16), ring(along_y, second).astype(BF16)
    first, second, out = lax.optimization_barrier((first, second, out))
    output = join_columns(place, x_exchange(out))
    grad_weight = second_phase(first, second, place).T
    grad_query, grad_key, grad_value = token_grads
    return (output[None], grad_query[None], grad_key[None], grad_value[None], grad_weight)


def solution(mesh):
    fine = Mesh(np.asarray(mesh.devices).reshape(2, NX, 2, 2, 4), AXES)
    dp = ("zl", "x", "c")
    return jax.shard_map(
        on_device,
        mesh=fine,
        in_specs=(
            P(dp, SEQ, None),
            P(dp, SEQ, None),
            P(dp, SEQ, None),
            P(SEQ, None),
            P(dp, SEQ, None),
            P(dp, SEQ),
            P(dp, None),
        ),
        out_specs=(
            P(dp, SEQ, None),
            P(dp, SEQ, None),
            P(dp, SEQ, None),
            P(dp, SEQ, None),
            P(SEQ, dp),
        ),
        check_vma=False,
    )
```

```python
import functools
import math

import jax
import jax.numpy as jnp
import numpy as np
from jax import lax
from jax.experimental import pallas as pl
from jax.experimental.pallas import tpu as pltpu
from jax.sharding import Mesh, PartitionSpec as P

HEAD_DIM = 128
HEADS = 3
GROUP = HEADS * HEAD_DIM
CAP = 160
TOK = 256
NS = 8
NX = 4
D = 5120
HALF = D // (2 * NX)
ROWS = NS * CAP
XROWS = NX * CAP
VMEM = 56 * 1024 * 1024
F32 = jnp.float32
BF16 = jnp.bfloat16
BRIEF = pl.CostEstimate(flops=1, bytes_accessed=1, transcendentals=0)
LONG = pl.CostEstimate(flops=2 * 10**11, bytes_accessed=1, transcendentals=0)
AXES = ("zl", "x", "c", "zh", "y")
SEQ = ("zh", "y")


def params(*semantics):
    return pltpu.CompilerParams(dimension_semantics=semantics, vmem_limit_bytes=VMEM)


def dot(a, b, dims):
    return lax.dot_general(a, b, (dims, ((), ())), preferred_element_type=F32)


def gather_kernel(pick_ref, q_ref, k_ref, v_ref, out_ref):
    token = lax.broadcasted_iota(jnp.int32, (CAP, TOK), 1)
    hot = (token == pick_ref[...]).astype(F32).astype(BF16)
    for i, ref in enumerate((q_ref, k_ref, v_ref)):
        rows = dot(hot, ref[...], ((1,), (0,))).astype(BF16)
        for s in range(2):
            out_ref[s, i] = rows[:, s * GROUP : (s + 1) * GROUP]


def gather_rows(pick, q, k, v):
    block = pl.BlockSpec((TOK, 2 * GROUP), lambda s: (0, s))
    return pl.pallas_call(
        gather_kernel,
        grid=(NS // 2,),
        in_specs=[pl.BlockSpec((CAP, 1), lambda s: (0, 0)), block, block, block],
        out_specs=pl.BlockSpec((2, 3, CAP, GROUP), lambda s: (s, 0, 0, 0)),
        out_shape=jax.ShapeDtypeStruct((NS, 3, CAP, GROUP), BF16),
        compiler_params=params("arbitrary"),
        cost_estimate=BRIEF,
    )(pick, q, k, v)


def scatter_kernel(pick_ref, first_ref, rest_ref, q_ref, k_ref, v_ref):
    token = lax.broadcasted_iota(jnp.int32, (TOK, CAP), 0)
    hot = (token == pick_ref[...]).astype(F32).astype(BF16)
    for i, ref in enumerate((q_ref, k_ref, v_ref)):
        rows = [part[s, i] for s in range(2) for part in (first_ref, rest_ref)]
        ref[...] = dot(hot, jnp.concatenate(rows, axis=1), ((1,), (0,))).astype(BF16)


def scatter_rows(pick, first, rest):
    block = pl.BlockSpec((TOK, 2 * GROUP), lambda s: (0, s))
    return pl.pallas_call(
        scatter_kernel,
        grid=(NS // 2,),
        in_specs=[
            pl.BlockSpec((1, CAP), lambda s: (0, 0)),
            pl.BlockSpec((2, 3, CAP, GROUP - HEAD_DIM), lambda s: (s, 0, 0, 0)),
            pl.BlockSpec((2, 3, CAP, HEAD_DIM), lambda s: (s, 0, 0, 0)),
        ],
        out_specs=[block] * 3,
        out_shape=[jax.ShapeDtypeStruct((TOK, NS * GROUP), BF16)] * 3,
        compiler_params=params("arbitrary"),
        cost_estimate=BRIEF,
    )(pick, first, rest)


QB = 4
NQ = NS // QB
COLUMN = pl.BlockSpec((QB, CAP, 1), lambda h, r: (r, 0, 0))
HEAD_COLUMN = pl.BlockSpec((1, QB, CAP, 1), lambda h, r: (h, r, 0, 0))
HEAD_ROWS = pl.BlockSpec((QB, CAP, HEAD_DIM), lambda h, r: (r, 0, h))
HEAD_SQUARE = pl.BlockSpec((1, QB * CAP, ROWS), lambda h, r: (h, r, 0))


def some_rows(i):
    return pl.BlockSpec((QB, 1, CAP, HEAD_DIM), lambda h, r: (r, i, 0, h))


def all_rows(i):
    return pl.BlockSpec((NS, 1, CAP, HEAD_DIM), lambda h, r: (0, i, 0, h))


def forward_kernel(bias_ref, live_ref, q_ref, k_ref, v_ref, attn_ref, expo_ref, inv_ref):
    scale = math.log2(math.e) / math.sqrt(HEAD_DIM)
    keys = k_ref[...].reshape(ROWS, HEAD_DIM)
    values = v_ref[...].reshape(ROWS, HEAD_DIM)
    bias = bias_ref[...]
    for j in range(QB):
        scores = dot(q_ref[j, 0], keys, ((1,), (1,))) + bias
        top = jnp.max(scores, axis=1, keepdims=True)
        expo = jnp.exp2((scores - top) * scale)
        inv = 1.0 / jnp.sum(expo, axis=1, keepdims=True)
        expo = expo.astype(BF16)
        expo_ref[0, j * CAP : (j + 1) * CAP, :] = expo
        inv_ref[0, j] = inv
        attn_ref[j] = (dot(expo, values, ((1,), (0,))) * (inv * live_ref[j])).astype(BF16)


def forward(bias, live, qkv):
    return pl.pallas_call(
        forward_kernel,
        grid=(HEADS, NQ),
        in_specs=[pl.BlockSpec((1, ROWS), lambda h, r: (0, 0)), COLUMN, some_rows(0), all_rows(1), all_rows(2)],
        out_specs=[HEAD_ROWS, HEAD_SQUARE, HEAD_COLUMN],
        out_shape=[
            jax.ShapeDtypeStruct((NS, CAP, GROUP), BF16),
            jax.ShapeDtypeStruct((HEADS, ROWS, ROWS), BF16),
            jax.ShapeDtypeStruct((HEADS, NS, CAP, 1), F32),
        ],
        compiler_params=params("arbitrary", "arbitrary"),
        cost_estimate=LONG,
    )(bias, live, qkv, qkv, qkv)


def backward_kernel(live_ref, q_ref, k_ref, v_ref, grad_ref, expo_ref, inv_ref, out_ref, gk_ref, gv_ref):
    r = pl.program_id(1)
    scale = 1.0 / math.sqrt(HEAD_DIM)
    keys = k_ref[...].reshape(ROWS, HEAD_DIM)
    values = v_ref[...].reshape(ROWS, HEAD_DIM)

    @pl.when(r == 0)
    def _():
        gk_ref[...] = jnp.zeros_like(gk_ref)
        gv_ref[...] = jnp.zeros_like(gv_ref)

    for j in range(QB):
        inv = inv_ref[0, j]
        grad = (grad_ref[j].astype(F32) * live_ref[j]).astype(BF16)
        expo_b = expo_ref[0, j * CAP : (j + 1) * CAP, :]
        expo = expo_b.astype(F32)
        dsoft = dot(grad, values, ((1,), (1,)))
        delta = jnp.sum(expo * dsoft, axis=1, keepdims=True) * inv
        dscore = (expo * ((dsoft - delta) * (inv * scale))).astype(BF16)
        out_ref[r * QB + j, 0] = dot(dscore, keys, ((1,), (0,))).astype(BF16)
        gv_ref[...] += dot((grad.astype(F32) * inv).astype(BF16), expo_b, ((0,), (0,)))
        gk_ref[...] += dot(q_ref[j, 0], dscore, ((0,), (0,)))

    @pl.when(r == NQ - 1)
    def _():
        out_ref[:, 1] = gk_ref[...].T.astype(BF16).reshape(NS, CAP, HEAD_DIM)
        out_ref[:, 2] = gv_ref[...].T.astype(BF16).reshape(NS, CAP, HEAD_DIM)


def backward(live, qkv, grad, expo, inv, first, count):
    def at(spec, axis):
        def index(h, r):
            place = list(spec.index_map(h, r))
            place[axis] = place[axis] + first
            return tuple(place)

        return pl.BlockSpec(spec.block_shape, index)

    rows = at(HEAD_ROWS, 2)
    return pl.pallas_call(
        backward_kernel,
        grid=(count, NQ),
        in_specs=[
            COLUMN,
            at(some_rows(0), 3),
            at(all_rows(1), 3),
            at(all_rows(2), 3),
            rows,
            at(HEAD_SQUARE, 0),
            at(HEAD_COLUMN, 0),
        ],
        out_specs=pl.BlockSpec((NS, 3, CAP, HEAD_DIM), lambda h, r: (0, 0, 0, h)),
        out_shape=jax.ShapeDtypeStruct((NS, 3, CAP, count * HEAD_DIM), BF16),
        scratch_shapes=[pltpu.VMEM((HEAD_DIM, ROWS), F32), pltpu.VMEM((HEAD_DIM, ROWS), F32)],
        compiler_params=params("arbitrary", "arbitrary"),
        cost_estimate=LONG,
    )(live, qkv, qkv, qkv, grad, expo, inv)


def column(place_ref, x, h):
    block = (h ^ place_ref[1]) * NX + x
    return pl.ds(pl.multiple_of(block * HALF, HALF), HALF)


def split_kernel(place_ref, in_ref, out_ref):
    for x in range(NX):
        for h in range(2):
            out_ref[x, h] = in_ref[:, column(place_ref, x, h)]


SMEM = pl.BlockSpec(memory_space=pltpu.SMEM)


def split_columns(place, rows):
    return pl.pallas_call(
        split_kernel,
        in_specs=[SMEM, pl.BlockSpec(memory_space=pltpu.VMEM)],
        out_specs=pl.BlockSpec(memory_space=pltpu.VMEM),
        out_shape=jax.ShapeDtypeStruct((NX, 2, CAP, HALF), BF16),
        compiler_params=params(),
        cost_estimate=BRIEF,
    )(place, rows)


def join_kernel(place_ref, in_ref, out_ref):
    for x in range(NX):
        for h in range(2):
            out_ref[:, column(place_ref, x, h)] = in_ref[x, h]


def join_columns(place, blocks):
    return pl.pallas_call(
        join_kernel,
        in_specs=[SMEM, pl.BlockSpec(memory_space=pltpu.VMEM)],
        out_specs=pl.BlockSpec(memory_space=pltpu.VMEM),
        out_shape=jax.ShapeDtypeStruct((CAP, D), BF16),
        compiler_params=params(),
        cost_estimate=BRIEF,
    )(place, blocks)


def x_exchange(blocks):
    return lax.all_to_all(blocks, "x", split_axis=0, concat_axis=0, tiled=True)


def whole_block(shape):
    return pl.BlockSpec(shape, lambda s, place: (0,) * len(shape))


LOW = GROUP // 2
UPPER = pl.BlockSpec((1, LOW, HALF), lambda s, place: (s, 0, 0))
LOWER = pl.BlockSpec((2, 1, LOW, HALF), lambda s, place: (0, s, 0, 0))
PAIR = pl.BlockSpec((NX, 2, 1, CAP, GROUP), lambda s, place: (0, 0, s, 0, 0))


def weight_rows(up, far, low):
    return jnp.concatenate([up[0], low[0, 0], far[0], low[1, 0]], axis=0)


def grad_attn_kernel(place_ref, in_ref, u0, f0, l0, u1, f1, l1, out_ref, cot_ref):
    @pl.when(pl.program_id(0) == 0)
    def _():
        for j in range(NX):
            for h in range(2):
                cot_ref[h, j * CAP : (j + 1) * CAP] = in_ref[j, h]

    total = dot(cot_ref[0], weight_rows(u0, f0, l0), ((1,), (1,)))
    total = (total + dot(cot_ref[1], weight_rows(u1, f1, l1), ((1,), (1,)))).astype(BF16)
    for j in range(NX):
        for i in range(2):
            part = total[j * CAP : (j + 1) * CAP, i * GROUP : (i + 1) * GROUP]
            out_ref[j, place_ref[2] ^ i, 0] = part


def grad_attn_part(place, cot, pieces):
    return pl.pallas_call(
        grad_attn_kernel,
        grid_spec=pltpu.PrefetchScalarGridSpec(
            num_scalar_prefetch=1,
            grid=(NS // 2,),
            in_specs=[whole_block((NX, 2, CAP, HALF))] + [UPPER, UPPER, LOWER] * 2,
            out_specs=PAIR,
            scratch_shapes=[pltpu.VMEM((2, XROWS, HALF), BF16)],
        ),
        out_shape=jax.ShapeDtypeStruct((NX, 2, NS // 2, CAP, GROUP), BF16),
        compiler_params=params("arbitrary"),
        cost_estimate=LONG,
    )(place, cot, *pieces).reshape(NX, NS, CAP, GROUP)


def ring_rows(ref, i):
    return ref[:, i, 0].reshape(XROWS, GROUP)


PIECE = HALF // 4


def weight_kernel(place_ref, attn_ref, cot_ref, keep_ref, send_ref, turn_ref):
    core = place_ref[1]

    @pl.when(pl.program_id(0) == 0)
    def _():
        for h in range(2):
            for j in range(NX):
                turned = cot_ref[j, h].T
                for c in range(2):
                    part = turned[2 * c * PIECE : 2 * (c + 1) * PIECE]
                    turn_ref[c ^ core, h ^ core, :, j * CAP : (j + 1) * CAP] = part

    rows = jnp.concatenate([ring_rows(attn_ref, i) for i in range(2)], axis=1)
    for other, ref in enumerate((keep_ref, send_ref)):
        for zl in range(2):
            total = dot(turn_ref[other, zl], rows, ((1,), (0,))).astype(BF16)
            for i in range(2):
                for p in range(2):
                    ref[p, zl, i, 0] = total[p * PIECE : (p + 1) * PIECE, i * GROUP : (i + 1) * GROUP]


def weight_part(place, attn, cot):
    grad = pl.BlockSpec((2, 2, 2, 1, PIECE, GROUP), lambda s, place: (0, 0, 0, s, 0, 0))
    return pl.pallas_call(
        weight_kernel,
        grid_spec=pltpu.PrefetchScalarGridSpec(
            num_scalar_prefetch=1,
            grid=(NS // 2,),
            in_specs=[PAIR, whole_block((NX, 2, CAP, HALF))],
            out_specs=[grad, grad],
            scratch_shapes=[pltpu.VMEM((2, 2, 2 * PIECE, XROWS), BF16)],
        ),
        out_shape=[jax.ShapeDtypeStruct((2, 2, 2, NS // 2, PIECE, GROUP), BF16)] * 2,
        compiler_params=params("arbitrary"),
        cost_estimate=BRIEF,
    )(place, attn, cot)


def out_kernel(place_ref, attn_ref, u0, f0, l0, u1, f1, l1, out_ref, acc_ref):
    s = pl.program_id(0)

    @pl.when(s == 0)
    def _():
        acc_ref[...] = jnp.zeros_like(acc_ref)

    rows = jnp.concatenate([ring_rows(attn_ref, place_ref[2] ^ i) for i in range(2)], axis=1)
    acc_ref[0] += dot(rows, weight_rows(u0, f0, l0), ((1,), (0,)))
    acc_ref[1] += dot(rows, weight_rows(u1, f1, l1), ((1,), (0,)))

    @pl.when(s == NS // 2 - 1)
    def _():
        for j in range(NX):
            for h in range(2):
                out_ref[j, h] = acc_ref[h, j * CAP : (j + 1) * CAP].astype(BF16)


def out_part(place, attn, pieces):
    return pl.pallas_call(
        out_kernel,
        grid_spec=pltpu.PrefetchScalarGridSpec(
            num_scalar_prefetch=1,
            grid=(NS // 2,),
            in_specs=[PAIR] + [UPPER, UPPER, LOWER] * 2,
            out_specs=whole_block((NX, 2, CAP, HALF)),
            scratch_shapes=[pltpu.VMEM((2, XROWS, HALF), F32)],
        ),
        out_shape=jax.ShapeDtypeStruct((NX, 2, CAP, HALF), BF16),
        compiler_params=params("arbitrary"),
        cost_estimate=BRIEF,
    )(place, attn, *pieces)


def other_core(value):
    return lax.ppermute(value, "c", [(0, 1), (1, 0)])


def swap(value):
    return lax.all_to_all(value, SEQ, split_axis=0, concat_axis=0, tiled=True)


def after(value, *others):
    return lax.optimization_barrier((value,) + others)[0]


def along_y(value, k):
    return lax.ppermute(value, "y", [(p, (p + k) % 4) for p in range(4)])


def along_z(value, k):
    index = [0, 2, 1, 3]
    return lax.ppermute(value, ("zl", "zh"), [(index[z], index[(z + k) % 4]) for z in range(4)])


def next_half(value):
    return lax.ppermute(value, ("zl", "zh"), [(0, 3), (3, 0), (2, 1), (1, 2)])


def add(values):
    return functools.reduce(jnp.add, [v.astype(F32) for v in values])


def projection(out_weight, x, core, y, rows):
    mine = lax.dynamic_slice(out_weight, (0, core * (NX * HALF) + x * HALF), (GROUP, HALF))

    def gather(value):
        parts = [value] + [along_y(value, k) for k in (1, 3, 2)]
        zero = jnp.zeros((4,) + value.shape, BF16)
        for k, part in zip((0, -1, 1, 2), parts):
            zero = lax.dynamic_update_slice_in_dim(zero, part[None], (y + k) % 4, 0)
        return zero

    up = gather(mine[:LOW])
    low = jnp.stack([mine[LOW:], next_half(mine[LOW:])])
    up, low, rows = lax.optimization_barrier((up, low, rows))
    far = next_half(up)
    low = jnp.moveaxis(gather(low), 0, 1)
    return [up, far, low], rows


def cut_kernel(place_ref, keep_ref, got_ref, z0, z1, z2, z3, y0, y1, y2, y3):
    for k, (z_ref, y_ref) in enumerate(zip((z0, z1, z2, z3), (y0, y1, y2, y3))):
        z = lax.rem(2 * place_ref[2] + place_ref[4] + k, 4)
        zl, zh, y = lax.rem(z, 2), z // 2, lax.rem(place_ref[3] + k, 4)
        z_ref[...] = (keep_ref[0, zl, zh].astype(F32) + got_ref[0, zl, zh].astype(F32)).astype(BF16)
        for i in range(2):
            for j in range(2):
                y_ref[i, j] = (keep_ref[1, i, j, y].astype(F32) + got_ref[1, i, j, y].astype(F32)).astype(BF16)


def cut_pieces(place, keep, got):
    vmem = pl.BlockSpec(memory_space=pltpu.VMEM)
    out = pl.pallas_call(
        cut_kernel,
        in_specs=[SMEM, vmem, vmem],
        out_specs=[vmem] * 8,
        out_shape=[jax.ShapeDtypeStruct((4, PIECE, GROUP), BF16)] * 4
        + [jax.ShapeDtypeStruct((2, 2, PIECE, GROUP), BF16)] * 4,
        compiler_params=params(),
        cost_estimate=BRIEF,
    )(place, keep, got)
    return out[:4], out[4:]


def ring(along, parts):
    return add([parts[0]] + [along(parts[k], k) for k in (1, 3, 2)])


def second_phase(first, second, place):
    zh, y, zl = place[2], place[3], place[4]
    first = [lax.dynamic_index_in_dim(first, (y + k) % 4, 0, keepdims=False) for k in range(4)]
    z = [(2 * zh + zl + k) % 4 for k in range(4)]
    second = [lax.dynamic_slice(second, (k % 2, k // 2, 0, 0), (1, 1, PIECE, GROUP))[0, 0] for k in z]
    return jnp.concatenate([ring(along_y, first), ring(along_z, second)])


def on_device(query_all, key_all, value_all, out_weight, cotangent, visible, counts):
    x, core, zh, y, zl = [lax.axis_index(a).astype(jnp.int32) for a in ("x", "c", "zh", "y", "zl")]
    place = jnp.stack([x, core, zh, y, zl])
    shard = 4 * zh + y

    slots = jnp.arange(CAP, dtype=jnp.int32)
    alive_all = slots[None, :] < counts[0][:, None]
    own_count = jnp.sum(jnp.where(jnp.arange(NS, dtype=jnp.int32) == shard, counts[0], 0))
    pick = jnp.where(slots < own_count, visible[0], -1)
    bias = jnp.where(alive_all, 0.0, -1e30).astype(F32).reshape(1, ROWS)
    live = alive_all.astype(F32)[:, :, None]

    rows = gather_rows(pick[:, None], query_all[0], key_all[0], value_all[0])
    own, rows = projection(out_weight, x, core, y, rows)
    cot = x_exchange(split_columns(place, after(cotangent[0], rows)))
    own = [after(v, cot) for v in own]
    qkv = swap(after(rows, cot, *own))
    pieces = own + [other_core(v) for v in own]
    grad_part = grad_attn_part(place, cot, pieces)
    grad_attn = swap(lax.psum_scatter(grad_part, "x", scatter_dimension=0, tiled=False))

    attn, expo, inv = forward(bias, live, after(qkv, grad_part))
    attn = lax.all_gather(swap(attn), "x", axis=0, tiled=False).reshape(NX, 2, NS // 2, CAP, GROUP)

    head_grads = backward(live, qkv, grad_attn, expo, inv, 0, HEADS - 1)
    grads = backward(after(live, head_grads), qkv, grad_attn, expo, inv, HEADS - 1, 1)
    keep, send = weight_part(place, after(attn, grads), cot)
    head_grads = swap(head_grads)
    grads = swap(grads)
    first, second = cut_pieces(place, keep, other_core(after(send, head_grads)))
    token_grads = scatter_rows(pick[None, :], head_grads, grads)
    out = out_part(place, after(attn, *first, *second), pieces)
    first = [*first[:2], after(first[2], out), first[3]]
    first, second = ring(along_z, first).astype(BF16), ring(along_y, second).astype(BF16)
    out = after(out, second, *token_grads)
    output = join_columns(place, x_exchange(out))
    grad_weight = second_phase(first, second, place).T
    grad_query, grad_key, grad_value = token_grads
    return (output[None], grad_query[None], grad_key[None], grad_value[None], grad_weight)


def solution(mesh):
    fine = Mesh(np.asarray(mesh.devices).reshape(2, NX, 2, 2, 4), AXES)
    dp = ("zl", "x", "c")
    return jax.shard_map(
        on_device,
        mesh=fine,
        in_specs=(
            P(dp, SEQ, None),
            P(dp, SEQ, None),
            P(dp, SEQ, None),
            P(SEQ, None),
            P(dp, SEQ, None),
            P(dp, SEQ),
            P(dp, None),
        ),
        out_specs=(
            P(dp, SEQ, None),
            P(dp, SEQ, None),
            P(dp, SEQ, None),
            P(dp, SEQ, None),
            P(SEQ, dp),
        ),
        check_vma=False,
    )
```

```python
import functools
import math

import jax
import jax.numpy as jnp
import numpy as np
from jax import lax
from jax.experimental import pallas as pl
from jax.experimental.pallas import tpu as pltpu
from jax.sharding import Mesh, PartitionSpec as P

HEAD_DIM = 128
HEADS = 3
GROUP = HEADS * HEAD_DIM
CAP = 160
TOK = 256
NS = 8
NX = 4
D = 5120
HALF = D // (2 * NX)
ROWS = NS * CAP
XROWS = NX * CAP
VMEM = 56 * 1024 * 1024
F32 = jnp.float32
BF16 = jnp.bfloat16
BRIEF = pl.CostEstimate(flops=1, bytes_accessed=1, transcendentals=0)
LONG = pl.CostEstimate(flops=2 * 10**11, bytes_accessed=1, transcendentals=0)
AXES = ("zl", "x", "c", "zh", "y")
SEQ = ("zh", "y")


def params(*semantics):
    return pltpu.CompilerParams(dimension_semantics=semantics, vmem_limit_bytes=VMEM)


def dot(a, b, dims):
    return lax.dot_general(a, b, (dims, ((), ())), preferred_element_type=F32)


def gather_kernel(pick_ref, q_ref, k_ref, v_ref, out_ref):
    token = lax.broadcasted_iota(jnp.int32, (CAP, TOK), 1)
    hot = (token == pick_ref[...]).astype(F32).astype(BF16)
    for i, ref in enumerate((q_ref, k_ref, v_ref)):
        rows = dot(hot, ref[...], ((1,), (0,))).astype(BF16)
        for s in range(2):
            out_ref[s, i] = rows[:, s * GROUP : (s + 1) * GROUP]


def gather_rows(pick, q, k, v):
    block = pl.BlockSpec((TOK, 2 * GROUP), lambda s: (0, s))
    return pl.pallas_call(
        gather_kernel,
        grid=(NS // 2,),
        in_specs=[pl.BlockSpec((CAP, 1), lambda s: (0, 0)), block, block, block],
        out_specs=pl.BlockSpec((2, 3, CAP, GROUP), lambda s: (s, 0, 0, 0)),
        out_shape=jax.ShapeDtypeStruct((NS, 3, CAP, GROUP), BF16),
        compiler_params=params("arbitrary"),
        cost_estimate=BRIEF,
    )(pick, q, k, v)


def scatter_kernel(pick_ref, first_ref, rest_ref, q_ref, k_ref, v_ref):
    token = lax.broadcasted_iota(jnp.int32, (TOK, CAP), 0)
    hot = (token == pick_ref[...]).astype(F32).astype(BF16)
    for i, ref in enumerate((q_ref, k_ref, v_ref)):
        rows = [part[s, i] for s in range(2) for part in (first_ref, rest_ref)]
        ref[...] = dot(hot, jnp.concatenate(rows, axis=1), ((1,), (0,))).astype(BF16)


def scatter_rows(pick, first, rest):
    block = pl.BlockSpec((TOK, 2 * GROUP), lambda s: (0, s))
    return pl.pallas_call(
        scatter_kernel,
        grid=(NS // 2,),
        in_specs=[
            pl.BlockSpec((1, CAP), lambda s: (0, 0)),
            pl.BlockSpec((2, 3, CAP, GROUP - HEAD_DIM), lambda s: (s, 0, 0, 0)),
            pl.BlockSpec((2, 3, CAP, HEAD_DIM), lambda s: (s, 0, 0, 0)),
        ],
        out_specs=[block] * 3,
        out_shape=[jax.ShapeDtypeStruct((TOK, NS * GROUP), BF16)] * 3,
        compiler_params=params("arbitrary"),
        cost_estimate=BRIEF,
    )(pick, first, rest)


QB = 4
NQ = NS // QB
COLUMN = pl.BlockSpec((QB, CAP, 1), lambda h, r: (r, 0, 0))
HEAD_COLUMN = pl.BlockSpec((1, QB, CAP, 1), lambda h, r: (h, r, 0, 0))
HEAD_ROWS = pl.BlockSpec((QB, CAP, HEAD_DIM), lambda h, r: (r, 0, h))
HEAD_SQUARE = pl.BlockSpec((1, QB * CAP, ROWS), lambda h, r: (h, r, 0))


def some_rows(i):
    return pl.BlockSpec((QB, 1, CAP, HEAD_DIM), lambda h, r: (r, i, 0, h))


def all_rows(i):
    return pl.BlockSpec((NS, 1, CAP, HEAD_DIM), lambda h, r: (0, i, 0, h))


def forward_kernel(bias_ref, live_ref, q_ref, k_ref, v_ref, attn_ref, expo_ref, inv_ref):
    scale = math.log2(math.e) / math.sqrt(HEAD_DIM)
    keys = k_ref[...].reshape(ROWS, HEAD_DIM)
    values = v_ref[...].reshape(ROWS, HEAD_DIM)
    bias = bias_ref[...]
    for j in range(QB):
        scores = dot(q_ref[j, 0], keys, ((1,), (1,))) + bias
        top = jnp.max(scores, axis=1, keepdims=True)
        expo = jnp.exp2((scores - top) * scale)
        inv = 1.0 / jnp.sum(expo, axis=1, keepdims=True)
        expo = expo.astype(BF16)
        expo_ref[0, j * CAP : (j + 1) * CAP, :] = expo
        inv_ref[0, j] = inv
        attn_ref[j] = (dot(expo, values, ((1,), (0,))) * (inv * live_ref[j])).astype(BF16)


def forward(bias, live, qkv):
    return pl.pallas_call(
        forward_kernel,
        grid=(HEADS, NQ),
        in_specs=[pl.BlockSpec((1, ROWS), lambda h, r: (0, 0)), COLUMN, some_rows(0), all_rows(1), all_rows(2)],
        out_specs=[HEAD_ROWS, HEAD_SQUARE, HEAD_COLUMN],
        out_shape=[
            jax.ShapeDtypeStruct((NS, CAP, GROUP), BF16),
            jax.ShapeDtypeStruct((HEADS, ROWS, ROWS), BF16),
            jax.ShapeDtypeStruct((HEADS, NS, CAP, 1), F32),
        ],
        compiler_params=params("arbitrary", "arbitrary"),
        cost_estimate=LONG,
    )(bias, live, qkv, qkv, qkv)


def backward_kernel(live_ref, q_ref, k_ref, v_ref, grad_ref, expo_ref, inv_ref, out_ref, gk_ref, gv_ref):
    r = pl.program_id(1)
    scale = 1.0 / math.sqrt(HEAD_DIM)
    keys = k_ref[...].reshape(ROWS, HEAD_DIM)
    values = v_ref[...].reshape(ROWS, HEAD_DIM)

    @pl.when(r == 0)
    def _():
        gk_ref[...] = jnp.zeros_like(gk_ref)
        gv_ref[...] = jnp.zeros_like(gv_ref)

    for j in range(QB):
        inv = inv_ref[0, j]
        grad = (grad_ref[j].astype(F32) * live_ref[j]).astype(BF16)
        expo_b = expo_ref[0, j * CAP : (j + 1) * CAP, :]
        expo = expo_b.astype(F32)
        dsoft = dot(grad, values, ((1,), (1,)))
        delta = jnp.sum(expo * dsoft, axis=1, keepdims=True) * inv
        dscore = (expo * ((dsoft - delta) * (inv * scale))).astype(BF16)
        out_ref[r * QB + j, 0] = dot(dscore, keys, ((1,), (0,))).astype(BF16)
        gv_ref[...] += dot((grad.astype(F32) * inv).astype(BF16), expo_b, ((0,), (0,)))
        gk_ref[...] += dot(q_ref[j, 0], dscore, ((0,), (0,)))

    @pl.when(r == NQ - 1)
    def _():
        out_ref[:, 1] = gk_ref[...].T.astype(BF16).reshape(NS, CAP, HEAD_DIM)
        out_ref[:, 2] = gv_ref[...].T.astype(BF16).reshape(NS, CAP, HEAD_DIM)


def backward(live, qkv, grad, expo, inv, first, count):
    def at(spec, axis):
        def index(h, r):
            place = list(spec.index_map(h, r))
            place[axis] = place[axis] + first
            return tuple(place)

        return pl.BlockSpec(spec.block_shape, index)

    rows = at(HEAD_ROWS, 2)
    return pl.pallas_call(
        backward_kernel,
        grid=(count, NQ),
        in_specs=[
            COLUMN,
            at(some_rows(0), 3),
            at(all_rows(1), 3),
            at(all_rows(2), 3),
            rows,
            at(HEAD_SQUARE, 0),
            at(HEAD_COLUMN, 0),
        ],
        out_specs=pl.BlockSpec((NS, 3, CAP, HEAD_DIM), lambda h, r: (0, 0, 0, h)),
        out_shape=jax.ShapeDtypeStruct((NS, 3, CAP, count * HEAD_DIM), BF16),
        scratch_shapes=[pltpu.VMEM((HEAD_DIM, ROWS), F32), pltpu.VMEM((HEAD_DIM, ROWS), F32)],
        compiler_params=params("arbitrary", "arbitrary"),
        cost_estimate=LONG,
    )(live, qkv, qkv, qkv, grad, expo, inv)


def column(place_ref, x, h):
    block = (h ^ place_ref[1]) * NX + x
    return pl.ds(pl.multiple_of(block * HALF, HALF), HALF)


def split_kernel(place_ref, in_ref, out_ref):
    for x in range(NX):
        for h in range(2):
            out_ref[x, h] = in_ref[:, column(place_ref, x, h)]


SMEM = pl.BlockSpec(memory_space=pltpu.SMEM)


def split_columns(place, rows):
    return pl.pallas_call(
        split_kernel,
        in_specs=[SMEM, pl.BlockSpec(memory_space=pltpu.VMEM)],
        out_specs=pl.BlockSpec(memory_space=pltpu.VMEM),
        out_shape=jax.ShapeDtypeStruct((NX, 2, CAP, HALF), BF16),
        compiler_params=params(),
        cost_estimate=BRIEF,
    )(place, rows)


def join_kernel(place_ref, in_ref, out_ref):
    for x in range(NX):
        for h in range(2):
            out_ref[:, column(place_ref, x, h)] = in_ref[x, h]


def join_columns(place, blocks):
    return pl.pallas_call(
        join_kernel,
        in_specs=[SMEM, pl.BlockSpec(memory_space=pltpu.VMEM)],
        out_specs=pl.BlockSpec(memory_space=pltpu.VMEM),
        out_shape=jax.ShapeDtypeStruct((CAP, D), BF16),
        compiler_params=params(),
        cost_estimate=BRIEF,
    )(place, blocks)


def x_exchange(blocks):
    return lax.all_to_all(blocks, "x", split_axis=0, concat_axis=0, tiled=True)


def whole_block(shape):
    return pl.BlockSpec(shape, lambda s, place: (0,) * len(shape))


LOW = GROUP // 2
UPPER = pl.BlockSpec((1, LOW, HALF), lambda s, place: (s, 0, 0))
LOWER = pl.BlockSpec((2, 1, LOW, HALF), lambda s, place: (0, s, 0, 0))
PAIR = pl.BlockSpec((NX, 2, 1, CAP, GROUP), lambda s, place: (0, 0, s, 0, 0))


def weight_rows(up, far, low):
    return jnp.concatenate([up[0], low[0, 0], far[0], low[1, 0]], axis=0)


PIECE = HALF // 4
TURNED = (2, 2, 2 * PIECE, XROWS)


def grad_attn_kernel(place_ref, in_ref, u0, f0, l0, u1, f1, l1, out_ref, turn_ref, cot_ref):
    core = place_ref[1]

    @pl.when(pl.program_id(0) == 0)
    def _():
        for j in range(NX):
            for h in range(2):
                cot_ref[h, j * CAP : (j + 1) * CAP] = in_ref[j, h]
                turned = in_ref[j, h].T
                for c in range(2):
                    part = turned[2 * c * PIECE : 2 * (c + 1) * PIECE]
                    turn_ref[c ^ core, h ^ core, :, j * CAP : (j + 1) * CAP] = part

    total = dot(cot_ref[0], weight_rows(u0, f0, l0), ((1,), (1,)))
    total = (total + dot(cot_ref[1], weight_rows(u1, f1, l1), ((1,), (1,)))).astype(BF16)
    for j in range(NX):
        for i in range(2):
            part = total[j * CAP : (j + 1) * CAP, i * GROUP : (i + 1) * GROUP]
            out_ref[j, place_ref[2] ^ i, 0] = part


def grad_attn_part(place, cot, pieces):
    part, turned = pl.pallas_call(
        grad_attn_kernel,
        grid_spec=pltpu.PrefetchScalarGridSpec(
            num_scalar_prefetch=1,
            grid=(NS // 2,),
            in_specs=[whole_block((NX, 2, CAP, HALF))] + [UPPER, UPPER, LOWER] * 2,
            out_specs=[PAIR, whole_block(TURNED)],
            scratch_shapes=[pltpu.VMEM((2, XROWS, HALF), BF16)],
        ),
        out_shape=[
            jax.ShapeDtypeStruct((NX, 2, NS // 2, CAP, GROUP), BF16),
            jax.ShapeDtypeStruct(TURNED, BF16),
        ],
        compiler_params=params("arbitrary"),
        cost_estimate=LONG,
    )(place, cot, *pieces)
    return part.reshape(NX, NS, CAP, GROUP), turned


def ring_rows(ref, i):
    return ref[:, i, 0].reshape(XROWS, GROUP)


def weight_kernel(attn_ref, turn_ref, keep_ref, send_ref):
    rows = jnp.concatenate([ring_rows(attn_ref, i) for i in range(2)], axis=1)
    for other, ref in enumerate((keep_ref, send_ref)):
        for zl in range(2):
            total = dot(turn_ref[other, zl], rows, ((1,), (0,))).astype(BF16)
            for i in range(2):
                for p in range(2):
                    ref[p, zl, i, 0] = total[p * PIECE : (p + 1) * PIECE, i * GROUP : (i + 1) * GROUP]


def weight_part(attn, turned):
    grad = pl.BlockSpec((2, 2, 2, 1, PIECE, GROUP), lambda s: (0, 0, 0, s, 0, 0))
    return pl.pallas_call(
        weight_kernel,
        grid=(NS // 2,),
        in_specs=[
            pl.BlockSpec((NX, 2, 1, CAP, GROUP), lambda s: (0, 0, s, 0, 0)),
            pl.BlockSpec(TURNED, lambda s: (0, 0, 0, 0)),
        ],
        out_specs=[grad, grad],
        out_shape=[jax.ShapeDtypeStruct((2, 2, 2, NS // 2, PIECE, GROUP), BF16)] * 2,
        compiler_params=params("arbitrary"),
        cost_estimate=BRIEF,
    )(attn, turned)


def out_kernel(place_ref, attn_ref, u0, f0, l0, u1, f1, l1, out_ref, acc_ref):
    s = pl.program_id(0)

    @pl.when(s == 0)
    def _():
        acc_ref[...] = jnp.zeros_like(acc_ref)

    rows = jnp.concatenate([ring_rows(attn_ref, place_ref[2] ^ i) for i in range(2)], axis=1)
    acc_ref[0] += dot(rows, weight_rows(u0, f0, l0), ((1,), (0,)))
    acc_ref[1] += dot(rows, weight_rows(u1, f1, l1), ((1,), (0,)))

    @pl.when(s == NS // 2 - 1)
    def _():
        for j in range(NX):
            for h in range(2):
                out_ref[j, h] = acc_ref[h, j * CAP : (j + 1) * CAP].astype(BF16)


def out_part(place, attn, pieces):
    return pl.pallas_call(
        out_kernel,
        grid_spec=pltpu.PrefetchScalarGridSpec(
            num_scalar_prefetch=1,
            grid=(NS // 2,),
            in_specs=[PAIR] + [UPPER, UPPER, LOWER] * 2,
            out_specs=whole_block((NX, 2, CAP, HALF)),
            scratch_shapes=[pltpu.VMEM((2, XROWS, HALF), F32)],
        ),
        out_shape=jax.ShapeDtypeStruct((NX, 2, CAP, HALF), BF16),
        compiler_params=params("arbitrary"),
        cost_estimate=BRIEF,
    )(place, attn, *pieces)


def other_core(value):
    return lax.ppermute(value, "c", [(0, 1), (1, 0)])


def swap(value):
    return lax.all_to_all(value, SEQ, split_axis=0, concat_axis=0, tiled=True)


def after(value, *others):
    return lax.optimization_barrier((value,) + others)[0]


def along_y(value, k):
    return lax.ppermute(value, "y", [(p, (p + k) % 4) for p in range(4)])


def along_z(value, k):
    index = [0, 2, 1, 3]
    return lax.ppermute(value, ("zl", "zh"), [(index[z], index[(z + k) % 4]) for z in range(4)])


def next_half(value):
    return lax.ppermute(value, ("zl", "zh"), [(0, 3), (3, 0), (2, 1), (1, 2)])


def add(values):
    return functools.reduce(jnp.add, [v.astype(F32) for v in values])


def projection(out_weight, x, core, y, rows):
    mine = lax.dynamic_slice(out_weight, (0, core * (NX * HALF) + x * HALF), (GROUP, HALF))

    def gather(value):
        parts = [value] + [along_y(value, k) for k in (1, 3, 2)]
        zero = jnp.zeros((4,) + value.shape, BF16)
        for k, part in zip((0, -1, 1, 2), parts):
            zero = lax.dynamic_update_slice_in_dim(zero, part[None], (y + k) % 4, 0)
        return zero

    up = gather(mine[:LOW])
    low = jnp.stack([mine[LOW:], next_half(mine[LOW:])])
    up, low, rows = lax.optimization_barrier((up, low, rows))
    far = next_half(up)
    low = jnp.moveaxis(gather(low), 0, 1)
    return [up, far, low], rows


def cut_kernel(place_ref, keep_ref, got_ref, z0, z1, z2, z3, y0, y1, y2, y3):
    z = 2 * pl.program_id(1) + pl.program_id(0)
    step = lax.rem(z + 4 - (2 * place_ref[2] + place_ref[4]), 4)
    for k, (z_ref, y_ref) in enumerate(zip((z0, z1, z2, z3), (y0, y1, y2, y3))):
        y = lax.rem(place_ref[3] + k, 4)
        y_ref[0, 0] = (keep_ref[1, 0, 0, y].astype(F32) + got_ref[1, 0, 0, y].astype(F32)).astype(BF16)

        @pl.when(step == k)
        def _():
            z_ref[...] = (keep_ref[0, 0, 0].astype(F32) + got_ref[0, 0, 0].astype(F32)).astype(BF16)


def cut_pieces(place, keep, got):
    piece = pl.BlockSpec((2, 1, 1, 4, PIECE, GROUP), lambda zl, zh, place: (0, zl, zh, 0, 0, 0))
    out = pl.pallas_call(
        cut_kernel,
        grid_spec=pltpu.PrefetchScalarGridSpec(
            num_scalar_prefetch=1,
            grid=(2, 2),
            in_specs=[piece, piece],
            out_specs=[pl.BlockSpec((4, PIECE, GROUP), lambda zl, zh, place: (0, 0, 0))] * 4
            + [pl.BlockSpec((1, 1, PIECE, GROUP), lambda zl, zh, place: (zl, zh, 0, 0))] * 4,
        ),
        out_shape=[jax.ShapeDtypeStruct((4, PIECE, GROUP), BF16)] * 4
        + [jax.ShapeDtypeStruct((2, 2, PIECE, GROUP), BF16)] * 4,
        compiler_params=params("arbitrary", "arbitrary"),
        cost_estimate=BRIEF,
    )(place, keep, got)
    return out[:4], out[4:]


def ring(along, parts):
    return add([parts[0]] + [along(parts[k], k) for k in (1, 3, 2)])


def second_phase(first, second, place):
    zh, y, zl = place[2], place[3], place[4]
    first = [lax.dynamic_index_in_dim(first, (y + k) % 4, 0, keepdims=False) for k in range(4)]
    z = [(2 * zh + zl + k) % 4 for k in range(4)]
    second = [lax.dynamic_slice(second, (k % 2, k // 2, 0, 0), (1, 1, PIECE, GROUP))[0, 0] for k in z]
    return jnp.concatenate([ring(along_y, first), ring(along_z, second)])


def on_device(query_all, key_all, value_all, out_weight, cotangent, visible, counts):
    x, core, zh, y, zl = [lax.axis_index(a).astype(jnp.int32) for a in ("x", "c", "zh", "y", "zl")]
    place = jnp.stack([x, core, zh, y, zl])
    shard = 4 * zh + y

    slots = jnp.arange(CAP, dtype=jnp.int32)
    alive_all = slots[None, :] < counts[0][:, None]
    own_count = jnp.sum(jnp.where(jnp.arange(NS, dtype=jnp.int32) == shard, counts[0], 0))
    pick = jnp.where(slots < own_count, visible[0], -1)
    bias = jnp.where(alive_all, 0.0, -1e30).astype(F32).reshape(1, ROWS)
    live = alive_all.astype(F32)[:, :, None]

    rows = gather_rows(pick[:, None], query_all[0], key_all[0], value_all[0])
    own, rows = projection(out_weight, x, core, y, rows)
    cot = x_exchange(split_columns(place, after(cotangent[0], rows)))
    own = [after(v, cot) for v in own]
    qkv = swap(after(rows, cot, *own))
    pieces = own + [other_core(v) for v in own]
    grad_part, turned = grad_attn_part(place, cot, pieces)
    grad_attn = swap(lax.psum_scatter(grad_part, "x", scatter_dimension=0, tiled=False))

    attn, expo, inv = forward(bias, live, after(qkv, grad_part))
    attn = lax.all_gather(swap(attn), "x", axis=0, tiled=False).reshape(NX, 2, NS // 2, CAP, GROUP)

    head_grads = backward(live, qkv, grad_attn, expo, inv, 0, HEADS - 1)
    grads = backward(after(live, head_grads), qkv, grad_attn, expo, inv, HEADS - 1, 1)
    keep, send = weight_part(after(attn, grads), turned)
    head_grads = swap(head_grads)
    grads = swap(grads)
    first, second = cut_pieces(place, keep, other_core(after(send, head_grads)))
    token_grads = scatter_rows(pick[None, :], head_grads, grads)
    out = out_part(place, after(attn, *first, *second), pieces)
    first = [*first[:2], after(first[2], out), first[3]]
    first, second = ring(along_z, first).astype(BF16), ring(along_y, second).astype(BF16)
    out = after(out, second, *token_grads)
    output = join_columns(place, x_exchange(out))
    grad_weight = second_phase(first, second, place).T
    grad_query, grad_key, grad_value = token_grads
    return (output[None], grad_query[None], grad_key[None], grad_value[None], grad_weight)


def solution(mesh):
    fine = Mesh(np.asarray(mesh.devices).reshape(2, NX, 2, 2, 4), AXES)
    dp = ("zl", "x", "c")
    return jax.shard_map(
        on_device,
        mesh=fine,
        in_specs=(
            P(dp, SEQ, None),
            P(dp, SEQ, None),
            P(dp, SEQ, None),
            P(SEQ, None),
            P(dp, SEQ, None),
            P(dp, SEQ),
            P(dp, None),
        ),
        out_specs=(
            P(dp, SEQ, None),
            P(dp, SEQ, None),
            P(dp, SEQ, None),
            P(dp, SEQ, None),
            P(SEQ, dp),
        ),
        check_vma=False,
    )
```

```python
import functools
import math

import jax
import jax.numpy as jnp
import numpy as np
from jax import lax
from jax.experimental import pallas as pl
from jax.experimental.pallas import tpu as pltpu
from jax.sharding import Mesh, PartitionSpec as P

HEAD_DIM = 128
HEADS = 3
GROUP = HEADS * HEAD_DIM
CAP = 160
TOK = 256
NS = 8
NX = 4
D = 5120
HALF = D // (2 * NX)
ROWS = NS * CAP
XROWS = NX * CAP
VMEM = 56 * 1024 * 1024
F32 = jnp.float32
BF16 = jnp.bfloat16
BRIEF = pl.CostEstimate(flops=1, bytes_accessed=1, transcendentals=0)
LONG = pl.CostEstimate(flops=2 * 10**11, bytes_accessed=1, transcendentals=0)
AXES = ("zl", "x", "c", "zh", "y")
SEQ = ("zh", "y")


def params(*semantics):
    return pltpu.CompilerParams(dimension_semantics=semantics, vmem_limit_bytes=VMEM)


def dot(a, b, dims):
    return lax.dot_general(a, b, (dims, ((), ())), preferred_element_type=F32)


def gather_kernel(pick_ref, q_ref, k_ref, v_ref, out_ref):
    token = lax.broadcasted_iota(jnp.int32, (CAP, TOK), 1)
    hot = (token == pick_ref[...]).astype(F32).astype(BF16)
    for i, ref in enumerate((q_ref, k_ref, v_ref)):
        rows = dot(hot, ref[...], ((1,), (0,))).astype(BF16)
        for s in range(2):
            out_ref[s, i] = rows[:, s * GROUP : (s + 1) * GROUP]


def gather_rows(pick, q, k, v):
    block = pl.BlockSpec((TOK, 2 * GROUP), lambda s: (0, s))
    return pl.pallas_call(
        gather_kernel,
        grid=(NS // 2,),
        in_specs=[pl.BlockSpec((CAP, 1), lambda s: (0, 0)), block, block, block],
        out_specs=pl.BlockSpec((2, 3, CAP, GROUP), lambda s: (s, 0, 0, 0)),
        out_shape=jax.ShapeDtypeStruct((NS, 3, CAP, GROUP), BF16),
        compiler_params=params("arbitrary"),
        cost_estimate=BRIEF,
    )(pick, q, k, v)


def scatter_kernel(pick_ref, first_ref, rest_ref, q_ref, k_ref, v_ref):
    token = lax.broadcasted_iota(jnp.int32, (TOK, CAP), 0)
    hot = (token == pick_ref[...]).astype(F32).astype(BF16)
    for i, ref in enumerate((q_ref, k_ref, v_ref)):
        rows = [part[s, i] for s in range(2) for part in (first_ref, rest_ref)]
        ref[...] = dot(hot, jnp.concatenate(rows, axis=1), ((1,), (0,))).astype(BF16)


def scatter_rows(pick, first, rest):
    block = pl.BlockSpec((TOK, 2 * GROUP), lambda s: (0, s))
    return pl.pallas_call(
        scatter_kernel,
        grid=(NS // 2,),
        in_specs=[
            pl.BlockSpec((1, CAP), lambda s: (0, 0)),
            pl.BlockSpec((2, 3, CAP, GROUP - HEAD_DIM), lambda s: (s, 0, 0, 0)),
            pl.BlockSpec((2, 3, CAP, HEAD_DIM), lambda s: (s, 0, 0, 0)),
        ],
        out_specs=[block] * 3,
        out_shape=[jax.ShapeDtypeStruct((TOK, NS * GROUP), BF16)] * 3,
        compiler_params=params("arbitrary"),
        cost_estimate=BRIEF,
    )(pick, first, rest)


QB = 4
NQ = NS // QB
COLUMN = pl.BlockSpec((QB, CAP, 1), lambda h, r: (r, 0, 0))
HEAD_COLUMN = pl.BlockSpec((1, QB, CAP, 1), lambda h, r: (h, r, 0, 0))
HEAD_ROWS = pl.BlockSpec((QB, CAP, HEAD_DIM), lambda h, r: (r, 0, h))
HEAD_SQUARE = pl.BlockSpec((1, QB * CAP, ROWS), lambda h, r: (h, r, 0))


def some_rows(i):
    return pl.BlockSpec((QB, 1, CAP, HEAD_DIM), lambda h, r: (r, i, 0, h))


def all_rows(i):
    return pl.BlockSpec((NS, 1, CAP, HEAD_DIM), lambda h, r: (0, i, 0, h))


def forward_kernel(bias_ref, live_ref, q_ref, k_ref, v_ref, attn_ref, expo_ref, inv_ref):
    scale = math.log2(math.e) / math.sqrt(HEAD_DIM)
    keys = k_ref[...].reshape(ROWS, HEAD_DIM)
    values = v_ref[...].reshape(ROWS, HEAD_DIM)
    bias = bias_ref[...]
    for j in range(QB):
        scores = dot(q_ref[j, 0], keys, ((1,), (1,))) + bias
        top = jnp.max(scores, axis=1, keepdims=True)
        expo = jnp.exp2((scores - top) * scale)
        inv = 1.0 / jnp.sum(expo, axis=1, keepdims=True)
        expo = expo.astype(BF16)
        expo_ref[0, j * CAP : (j + 1) * CAP, :] = expo
        inv_ref[0, j] = inv
        attn_ref[j] = (dot(expo, values, ((1,), (0,))) * (inv * live_ref[j])).astype(BF16)


def forward(bias, live, qkv):
    return pl.pallas_call(
        forward_kernel,
        grid=(HEADS, NQ),
        in_specs=[pl.BlockSpec((1, ROWS), lambda h, r: (0, 0)), COLUMN, some_rows(0), all_rows(1), all_rows(2)],
        out_specs=[HEAD_ROWS, HEAD_SQUARE, HEAD_COLUMN],
        out_shape=[
            jax.ShapeDtypeStruct((NS, CAP, GROUP), BF16),
            jax.ShapeDtypeStruct((HEADS, ROWS, ROWS), BF16),
            jax.ShapeDtypeStruct((HEADS, NS, CAP, 1), F32),
        ],
        compiler_params=params("arbitrary", "arbitrary"),
        cost_estimate=LONG,
    )(bias, live, qkv, qkv, qkv)


def backward_kernel(live_ref, q_ref, k_ref, v_ref, grad_ref, expo_ref, inv_ref, out_ref, gk_ref, gv_ref):
    r = pl.program_id(1)
    scale = 1.0 / math.sqrt(HEAD_DIM)
    keys = k_ref[...].reshape(ROWS, HEAD_DIM)
    values = v_ref[...].reshape(ROWS, HEAD_DIM)

    @pl.when(r == 0)
    def _():
        gk_ref[...] = jnp.zeros_like(gk_ref)
        gv_ref[...] = jnp.zeros_like(gv_ref)

    for j in range(QB):
        inv = inv_ref[0, j]
        grad = (grad_ref[j].astype(F32) * live_ref[j]).astype(BF16)
        expo_b = expo_ref[0, j * CAP : (j + 1) * CAP, :]
        expo = expo_b.astype(F32)
        dsoft = dot(grad, values, ((1,), (1,)))
        delta = jnp.sum(expo * dsoft, axis=1, keepdims=True) * inv
        dscore = (expo * ((dsoft - delta) * (inv * scale))).astype(BF16)
        out_ref[r * QB + j, 0] = dot(dscore, keys, ((1,), (0,))).astype(BF16)
        gv_ref[...] += dot((grad.astype(F32) * inv).astype(BF16), expo_b, ((0,), (0,)))
        gk_ref[...] += dot(q_ref[j, 0], dscore, ((0,), (0,)))

    @pl.when(r == NQ - 1)
    def _():
        out_ref[:, 1] = gk_ref[...].T.astype(BF16).reshape(NS, CAP, HEAD_DIM)
        out_ref[:, 2] = gv_ref[...].T.astype(BF16).reshape(NS, CAP, HEAD_DIM)


def backward(live, qkv, grad, expo, inv, first, count):
    def at(spec, axis):
        def index(h, r):
            place = list(spec.index_map(h, r))
            place[axis] = place[axis] + first
            return tuple(place)

        return pl.BlockSpec(spec.block_shape, index)

    rows = at(HEAD_ROWS, 2)
    return pl.pallas_call(
        backward_kernel,
        grid=(count, NQ),
        in_specs=[
            COLUMN,
            at(some_rows(0), 3),
            at(all_rows(1), 3),
            at(all_rows(2), 3),
            rows,
            at(HEAD_SQUARE, 0),
            at(HEAD_COLUMN, 0),
        ],
        out_specs=pl.BlockSpec((NS, 3, CAP, HEAD_DIM), lambda h, r: (0, 0, 0, h)),
        out_shape=jax.ShapeDtypeStruct((NS, 3, CAP, count * HEAD_DIM), BF16),
        scratch_shapes=[pltpu.VMEM((HEAD_DIM, ROWS), F32), pltpu.VMEM((HEAD_DIM, ROWS), F32)],
        compiler_params=params("arbitrary", "arbitrary"),
        cost_estimate=LONG,
    )(live, qkv, qkv, qkv, grad, expo, inv)


def column(place_ref, x, h):
    block = (h ^ place_ref[1]) * NX + x
    return pl.ds(pl.multiple_of(block * HALF, HALF), HALF)


def split_kernel(place_ref, in_ref, out_ref):
    for x in range(NX):
        for h in range(2):
            out_ref[x, h] = in_ref[:, column(place_ref, x, h)]


SMEM = pl.BlockSpec(memory_space=pltpu.SMEM)


def split_columns(place, rows):
    return pl.pallas_call(
        split_kernel,
        in_specs=[SMEM, pl.BlockSpec(memory_space=pltpu.VMEM)],
        out_specs=pl.BlockSpec(memory_space=pltpu.VMEM),
        out_shape=jax.ShapeDtypeStruct((NX, 2, CAP, HALF), BF16),
        compiler_params=params(),
        cost_estimate=BRIEF,
    )(place, rows)


def join_kernel(place_ref, in_ref, out_ref):
    for x in range(NX):
        for h in range(2):
            out_ref[:, column(place_ref, x, h)] = in_ref[x, h]


def join_columns(place, blocks):
    return pl.pallas_call(
        join_kernel,
        in_specs=[SMEM, pl.BlockSpec(memory_space=pltpu.VMEM)],
        out_specs=pl.BlockSpec(memory_space=pltpu.VMEM),
        out_shape=jax.ShapeDtypeStruct((CAP, D), BF16),
        compiler_params=params(),
        cost_estimate=BRIEF,
    )(place, blocks)


def x_exchange(blocks):
    return lax.all_to_all(blocks, "x", split_axis=0, concat_axis=0, tiled=True)


def whole_block(shape):
    return pl.BlockSpec(shape, lambda s, place: (0,) * len(shape))


LOW = GROUP // 2
UPPER = pl.BlockSpec((1, LOW, HALF), lambda s, place: (s, 0, 0))
LOWER = pl.BlockSpec((2, 1, LOW, HALF), lambda s, place: (0, s, 0, 0))
PAIR = pl.BlockSpec((NX, 2, 1, CAP, GROUP), lambda s, place: (0, 0, s, 0, 0))


def weight_rows(up, far, low):
    return jnp.concatenate([up[0], low[0, 0], far[0], low[1, 0]], axis=0)


PIECE = HALF // 4
TURNED = (2, 2, 2 * PIECE, XROWS)


def grad_attn_kernel(place_ref, in_ref, u0, f0, l0, u1, f1, l1, out_ref, turn_ref, cot_ref):
    core = place_ref[1]

    @pl.when(pl.program_id(0) == 0)
    def _():
        for j in range(NX):
            for h in range(2):
                cot_ref[h, j * CAP : (j + 1) * CAP] = in_ref[j, h]
                turned = in_ref[j, h].T
                for c in range(2):
                    part = turned[2 * c * PIECE : 2 * (c + 1) * PIECE]
                    turn_ref[c ^ core, h ^ core, :, j * CAP : (j + 1) * CAP] = part

    total = dot(cot_ref[0], weight_rows(u0, f0, l0), ((1,), (1,)))
    total = (total + dot(cot_ref[1], weight_rows(u1, f1, l1), ((1,), (1,)))).astype(BF16)
    for j in range(NX):
        for i in range(2):
            part = total[j * CAP : (j + 1) * CAP, i * GROUP : (i + 1) * GROUP]
            out_ref[j, place_ref[2] ^ i, 0] = part


def grad_attn_part(place, cot, pieces):
    part, turned = pl.pallas_call(
        grad_attn_kernel,
        grid_spec=pltpu.PrefetchScalarGridSpec(
            num_scalar_prefetch=1,
            grid=(NS // 2,),
            in_specs=[whole_block((NX, 2, CAP, HALF))] + [UPPER, UPPER, LOWER] * 2,
            out_specs=[PAIR, whole_block(TURNED)],
            scratch_shapes=[pltpu.VMEM((2, XROWS, HALF), BF16)],
        ),
        out_shape=[
            jax.ShapeDtypeStruct((NX, 2, NS // 2, CAP, GROUP), BF16),
            jax.ShapeDtypeStruct(TURNED, BF16),
        ],
        compiler_params=params("arbitrary"),
        cost_estimate=LONG,
    )(place, cot, *pieces)
    return part.reshape(NX, NS, CAP, GROUP), turned


def ring_rows(ref, i):
    return ref[:, i, 0].reshape(XROWS, GROUP)


def weight_kernel(attn_ref, turn_ref, keep_ref, send_ref):
    rows = jnp.concatenate([ring_rows(attn_ref, i) for i in range(2)], axis=1)
    for other, ref in enumerate((keep_ref, send_ref)):
        for zl in range(2):
            total = dot(turn_ref[other, zl], rows, ((1,), (0,))).astype(BF16)
            for i in range(2):
                for p in range(2):
                    ref[p, zl, i, 0] = total[p * PIECE : (p + 1) * PIECE, i * GROUP : (i + 1) * GROUP]


def weight_part(attn, turned):
    grad = pl.BlockSpec((2, 2, 2, 1, PIECE, GROUP), lambda s: (0, 0, 0, s, 0, 0))
    return pl.pallas_call(
        weight_kernel,
        grid=(NS // 2,),
        in_specs=[
            pl.BlockSpec((NX, 2, 1, CAP, GROUP), lambda s: (0, 0, s, 0, 0)),
            pl.BlockSpec(TURNED, lambda s: (0, 0, 0, 0)),
        ],
        out_specs=[grad, grad],
        out_shape=[jax.ShapeDtypeStruct((2, 2, 2, NS // 2, PIECE, GROUP), BF16)] * 2,
        compiler_params=params("arbitrary"),
        cost_estimate=BRIEF,
    )(attn, turned)


def out_kernel(place_ref, attn_ref, u0, f0, l0, u1, f1, l1, out_ref, acc_ref):
    s = pl.program_id(0)

    @pl.when(s == 0)
    def _():
        acc_ref[...] = jnp.zeros_like(acc_ref)

    rows = jnp.concatenate([ring_rows(attn_ref, place_ref[2] ^ i) for i in range(2)], axis=1)
    acc_ref[0] += dot(rows, weight_rows(u0, f0, l0), ((1,), (0,)))
    acc_ref[1] += dot(rows, weight_rows(u1, f1, l1), ((1,), (0,)))

    @pl.when(s == NS // 2 - 1)
    def _():
        for j in range(NX):
            for h in range(2):
                out_ref[j, h] = acc_ref[h, j * CAP : (j + 1) * CAP].astype(BF16)


def out_part(place, attn, pieces):
    return pl.pallas_call(
        out_kernel,
        grid_spec=pltpu.PrefetchScalarGridSpec(
            num_scalar_prefetch=1,
            grid=(NS // 2,),
            in_specs=[PAIR] + [UPPER, UPPER, LOWER] * 2,
            out_specs=whole_block((NX, 2, CAP, HALF)),
            scratch_shapes=[pltpu.VMEM((2, XROWS, HALF), F32)],
        ),
        out_shape=jax.ShapeDtypeStruct((NX, 2, CAP, HALF), BF16),
        compiler_params=params("arbitrary"),
        cost_estimate=BRIEF,
    )(place, attn, *pieces)


def other_core(value):
    return lax.ppermute(value, "c", [(0, 1), (1, 0)])


def swap(value):
    return lax.all_to_all(value, SEQ, split_axis=0, concat_axis=0, tiled=True)


def after(value, *others):
    return lax.optimization_barrier((value,) + others)[0]


def along_y(value, k):
    return lax.ppermute(value, "y", [(p, (p + k) % 4) for p in range(4)])


def along_z(value, k):
    index = [0, 2, 1, 3]
    return lax.ppermute(value, ("zl", "zh"), [(index[z], index[(z + k) % 4]) for z in range(4)])


def next_half(value):
    return lax.ppermute(value, ("zl", "zh"), [(0, 3), (3, 0), (2, 1), (1, 2)])


def add(values):
    return functools.reduce(jnp.add, [v.astype(F32) for v in values])


def projection(out_weight, x, core, y, rows):
    mine = lax.dynamic_slice(out_weight, (0, core * (NX * HALF) + x * HALF), (GROUP, HALF))

    def gather(value):
        parts = [value] + [along_y(value, k) for k in (1, 3, 2)]
        zero = jnp.zeros((4,) + value.shape, BF16)
        for k, part in zip((0, -1, 1, 2), parts):
            zero = lax.dynamic_update_slice_in_dim(zero, part[None], (y + k) % 4, 0)
        return zero

    up = gather(mine[:LOW])
    low = jnp.stack([mine[LOW:], next_half(mine[LOW:])])
    up, low, rows = lax.optimization_barrier((up, low, rows))
    far = next_half(up)
    low = jnp.moveaxis(gather(low), 0, 1)
    return [up, far, low], rows


def cut_kernel(place_ref, keep_ref, got_ref, z0, z1, z2, z3, y0, y1, y2, y3):
    z = 2 * pl.program_id(1) + pl.program_id(0)
    step = lax.rem(z + 4 - (2 * place_ref[2] + place_ref[4]), 4)
    for k, (z_ref, y_ref) in enumerate(zip((z0, z1, z2, z3), (y0, y1, y2, y3))):
        y = lax.rem(place_ref[3] + k, 4)
        y_ref[0, 0] = (keep_ref[1, 0, 0, y].astype(F32) + got_ref[1, 0, 0, y].astype(F32)).astype(BF16)

        @pl.when(step == k)
        def _():
            z_ref[...] = (keep_ref[0, 0, 0].astype(F32) + got_ref[0, 0, 0].astype(F32)).astype(BF16)


def cut_pieces(place, keep, got):
    piece = pl.BlockSpec((2, 1, 1, 4, PIECE, GROUP), lambda zl, zh, place: (0, zl, zh, 0, 0, 0))
    out = pl.pallas_call(
        cut_kernel,
        grid_spec=pltpu.PrefetchScalarGridSpec(
            num_scalar_prefetch=1,
            grid=(2, 2),
            in_specs=[piece, piece],
            out_specs=[pl.BlockSpec((4, PIECE, GROUP), lambda zl, zh, place: (0, 0, 0))] * 4
            + [pl.BlockSpec((1, 1, PIECE, GROUP), lambda zl, zh, place: (zl, zh, 0, 0))] * 4,
        ),
        out_shape=[jax.ShapeDtypeStruct((4, PIECE, GROUP), BF16)] * 4
        + [jax.ShapeDtypeStruct((2, 2, PIECE, GROUP), BF16)] * 4,
        compiler_params=params("arbitrary", "arbitrary"),
        cost_estimate=BRIEF,
    )(place, keep, got)
    return out[:4], out[4:]


def ring(along, parts):
    return add([parts[0]] + [along(parts[k], k) for k in (1, 3, 2)])


def second_phase(first, second, place):
    zh, y, zl = place[2], place[3], place[4]
    first = [lax.dynamic_index_in_dim(first, (y + k) % 4, 0, keepdims=False) for k in range(4)]
    z = [(2 * zh + zl + k) % 4 for k in range(4)]
    second = [lax.dynamic_slice(second, (k % 2, k // 2, 0, 0), (1, 1, PIECE, GROUP))[0, 0] for k in z]
    return jnp.concatenate([ring(along_y, first), ring(along_z, second)])


def on_device(query_all, key_all, value_all, out_weight, cotangent, visible, counts):
    x, core, zh, y, zl = [lax.axis_index(a).astype(jnp.int32) for a in ("x", "c", "zh", "y", "zl")]
    place = jnp.stack([x, core, zh, y, zl])
    shard = 4 * zh + y

    slots = jnp.arange(CAP, dtype=jnp.int32)
    alive_all = slots[None, :] < counts[0][:, None]
    own_count = jnp.sum(jnp.where(jnp.arange(NS, dtype=jnp.int32) == shard, counts[0], 0))
    pick = jnp.where(slots < own_count, visible[0], -1)
    bias = jnp.where(alive_all, 0.0, -1e30).astype(F32).reshape(1, ROWS)
    live = alive_all.astype(F32)[:, :, None]

    rows = gather_rows(pick[:, None], query_all[0], key_all[0], value_all[0])
    own, rows = projection(out_weight, x, core, y, rows)
    cot = x_exchange(split_columns(place, after(cotangent[0], rows)))
    own = [after(v, cot) for v in own]
    qkv = swap(after(rows, cot, *own))
    pieces = own + [other_core(v) for v in own]
    grad_part, turned = grad_attn_part(place, cot, pieces)
    grad_attn = swap(lax.psum_scatter(grad_part, "x", scatter_dimension=0, tiled=False))

    attn, expo, inv = forward(bias, live, after(qkv, grad_part))
    attn = lax.all_gather(swap(attn), "x", axis=0, tiled=False).reshape(NX, 2, NS // 2, CAP, GROUP)

    head_grads = backward(live, qkv, grad_attn, expo, inv, 0, HEADS - 1)
    grads = backward(after(live, head_grads), qkv, grad_attn, expo, inv, HEADS - 1, 1)
    keep, send = weight_part(after(attn, grads), turned)
    head_grads = swap(head_grads)
    grads = swap(grads)
    first, second = cut_pieces(place, keep, other_core(after(send, head_grads)))
    token_grads = scatter_rows(pick[None, :], head_grads, grads)
    out = out_part(place, after(attn, *first, *second), pieces)
    first = [*first[:2], after(first[2], out), first[3]]
    first, second = ring(along_z, first).astype(BF16), ring(along_y, second).astype(BF16)
    out = after(out, *token_grads)
    output = join_columns(place, x_exchange(out))
    grad_weight = second_phase(first, second, place).T
    grad_query, grad_key, grad_value = token_grads
    return (output[None], grad_query[None], grad_key[None], grad_value[None], grad_weight)


def solution(mesh):
    fine = Mesh(np.asarray(mesh.devices).reshape(2, NX, 2, 2, 4), AXES)
    dp = ("zl", "x", "c")
    return jax.shard_map(
        on_device,
        mesh=fine,
        in_specs=(
            P(dp, SEQ, None),
            P(dp, SEQ, None),
            P(dp, SEQ, None),
            P(SEQ, None),
            P(dp, SEQ, None),
            P(dp, SEQ),
            P(dp, None),
        ),
        out_specs=(
            P(dp, SEQ, None),
            P(dp, SEQ, None),
            P(dp, SEQ, None),
            P(dp, SEQ, None),
            P(SEQ, dp),
        ),
        check_vma=False,
    )
```
